768 devices in a mesh: outer: 192 (over z_lo, x, y, core), inner: 4 (over z_hi).
Axes of the slice: x: 4, y: 8, z: 12 (z_hi: 4, z_lo: 3; z = z_hi * 3 + z_lo), core: 2. Of those that a mesh axis runs over, the one named last changes fastest.
Arguments:
- images: bfloat16 [196608, 1152], P(('outer', 'inner')), may hold values from -0.625 to 0.625
- texts: bfloat16 [196608, 1152], P(('outer', 'inner')), may hold values from -0.625 to 0.625
- positive: int32 [196608], P(('outer', 'inner')), may hold values from 0 to 196607, as said below
- logit_scale: float32 [1], replicated, may hold values from 8 to 12
- logit_bias: float32 [1], replicated, may hold values from -8 to -5
Outputs:
- loss_rows: float32 [196608], P(('outer', 'inner'))
- image_grad: bfloat16 [196608, 1152], P(('outer', 'inner'))
- text_grad: bfloat16 [196608, 1152], P(('outer', 'inner'))
The draws below stay inside these ranges and needn't reach their ends.
Inputs may be any that keep to these rules, and one draw needn't show every extreme that they name: positive[i] lies in the window W(i) of image i: a text of its own group or of the group before it, cyclically; group size 1024.
All inputs are finite; a program needn't handle non-finite values.
Results may differ from the reference program's by a relative error of at most 0.0039.
Values may be sent and summed in bfloat16 or wider, within the bound.
No kernel may reach another device: no remote copies, remote signals or barrier semaphores. Data moves between devices by JAX's collectives and lax.ppermute only.
A program may use at most 64 MiB of HBM per device.

```python
import jax
import jax.numpy as jnp
from jax import lax

D = 1152
GROUP = 1024
TOKENS = 196608


def draw_positive(key, part):
    key = jax.random.fold_in(key, 5)
    offset = jax.random.randint(key, (TOKENS,), 0, 2 * GROUP, dtype=jnp.int32)
    groups = TOKENS // GROUP
    home = jnp.arange(TOKENS, dtype=jnp.int32) // GROUP
    target = (home - (offset >= GROUP).astype(jnp.int32) + groups) % groups
    return target * GROUP + offset % GROUP


def levels(own_key, extent, pieces, smallest, high):
    loudness, own = 1.0, jax.random.fold_in(own_key, 6)
    for dim, shards_of in pieces:
        heights = jnp.exp(jax.random.uniform(jax.random.fold_in(own, dim), (shards_of,), jnp.float32, smallest / len(pieces), high / len(pieces)))
        loudness = loudness * jnp.repeat(heights, extent[dim] // shards_of).reshape([-1 if axis == dim else 1 for axis in range(len(extent))])
    return loudness


def centred(key, shape, spread, limit, shards=(), kind=jnp.bfloat16):
    values = jax.random.normal(key, shape, jnp.float32) * spread
    if len(shards) > 0:
        values = levels(key, shape, shards, -0.22, 0.18) * values
    return jnp.clip(values, min=-limit, max=limit).astype(kind)


def setup_inputs(seed: int = 0) -> dict:
    seeds = jax.random.split(jax.random.key(seed), 6)
    return {
        "images": centred(seeds[0], (TOKENS, D), 0.1, 0.625, ((0, 768),)),
        "texts": centred(seeds[1], (TOKENS, D), 0.1, 0.625, ((0, 768),)),
        "positive": draw_positive(jax.random.fold_in(seeds[5], 71), 0),
        "logit_scale": jnp.clip(jax.random.uniform(seeds[3], (1,), jnp.float32, 8.0, 12.0), 8.0, 12.0),
        "logit_bias": jnp.clip(jax.random.uniform(seeds[4], (1,), jnp.float32, -8.0, -5.0), -8.0, -5.0),
    }


def reference(images, texts, positive, logit_scale, logit_bias):
    groups = TOKENS // GROUP
    scale = logit_scale[0]
    bias = logit_bias[0]
    img = images.reshape(groups, GROUP, D)
    txt = texts.reshape(groups, GROUP, D)
    prev_txt = jnp.roll(txt, 1, axis=0)
    pos = positive.reshape(groups, GROUP)
    order = jnp.arange(groups, dtype=jnp.int32)
    cols = jnp.arange(GROUP, dtype=jnp.int32)

    def one_group(items):
        block, own, prior, block_pos, index = items
        window = jnp.concatenate([own, prior], axis=0)
        ids = jnp.concatenate([index * GROUP + cols, ((index - 1 + groups) % groups) * GROUP + cols])
        hits = block_pos[:, None] == ids[None, :]
        logits = scale * lax.dot_general(block, window, (((1,), (1,)), ((), ())), preferred_element_type=jnp.float32) + bias
        signs = jnp.where(hits, 1.0, -1.0).astype(jnp.float32)
        loss = jnp.sum(jax.nn.softplus(-signs * logits), axis=1)
        weights = (jax.nn.sigmoid(logits) - hits.astype(jnp.float32)).astype(jnp.bfloat16)
        grad_img = (scale * jnp.dot(weights, window, preferred_element_type=jnp.float32)).astype(jnp.bfloat16)
        parts = lax.dot_general(weights, block, (((0,), (0,)), ((), ())), preferred_element_type=jnp.float32)
        return loss, grad_img, parts[:GROUP], parts[GROUP:]

    loss, grad_img, own_parts, prev_parts = lax.map(one_group, (img, txt, prev_txt, pos, order))
    grad_txt = (scale * (own_parts + jnp.roll(prev_parts, -1, axis=0))).astype(jnp.bfloat16)
    return loss.reshape(TOKENS), grad_img.reshape(TOKENS, D), grad_txt.reshape(TOKENS, D)
```

```python
import jax
import jax.numpy as jnp
from jax import lax
from jax.sharding import PartitionSpec as P

IMAGE_PAIRS = [(0, 1), (1, 0), (2, 3), (3, 2)]
TEXT_PAIRS = [(1, 2), (2, 1), (3, 0), (0, 3)]


def from_behind(block, distance):
    count = lax.axis_size("outer")
    return lax.ppermute(block, "outer", [((i - distance) % count, i) for i in range(count)])


def per_device(images, texts, positive, logit_scale, logit_bias):
    scale = logit_scale[0]
    bias = logit_bias[0]
    rows = texts.shape[0]
    count = lax.axis_size("outer")
    group = lax.axis_index("outer")
    me = lax.axis_index("inner")
    other = 3 - me
    there = lax.ppermute(positive, "inner", IMAGE_PAIRS)
    texts_there = lax.ppermute(texts, "inner", TEXT_PAIRS)
    images_there = lax.ppermute(images, "inner", IMAGE_PAIRS)
    prior = from_behind(texts, 1)
    prior_there = from_behind(texts_there, 1)

    image_pair = jnp.concatenate([images, images_there], axis=0)
    window = jnp.concatenate([texts, texts_there, prior, prior_there], axis=0)
    positives = jnp.concatenate([positive, there])
    width = 4 * rows
    before = (group - 1 + count) % count
    cols = jnp.arange(rows, dtype=jnp.int32)
    ids = jnp.concatenate(
        [
            group * width + me * rows + cols,
            group * width + other * rows + cols,
            before * width + me * rows + cols,
            before * width + other * rows + cols,
        ]
    )
    hits = positives[:, None] == ids[None, :]
    logits = (
        scale
        * lax.dot_general(
            image_pair, window, (((1,), (1,)), ((), ())), preferred_element_type=jnp.float32
        )
        + bias
    )
    signs = jnp.where(hits, 1.0, -1.0).astype(jnp.float32)
    losses = jnp.sum(jax.nn.softplus(-signs * logits), axis=1)
    weights = (jax.nn.sigmoid(logits) - hits.astype(jnp.float32)).astype(jnp.bfloat16)

    text_parts = lax.dot_general(
        weights, image_pair, (((0,), (0,)), ((), ())), preferred_element_type=jnp.float32
    )
    returned = from_behind(text_parts[2 * rows :].astype(jnp.bfloat16), -1)
    image_parts = jnp.dot(weights, window, preferred_element_type=jnp.float32)
    image_back = lax.ppermute(image_parts[rows:].astype(jnp.bfloat16), "inner", IMAGE_PAIRS)
    loss_back = lax.ppermute(losses[rows:], "inner", IMAGE_PAIRS)
    text_sum = text_parts[: 2 * rows] + returned.astype(jnp.float32)
    text_back = lax.ppermute(text_sum[rows:].astype(jnp.bfloat16), "inner", TEXT_PAIRS)

    loss_rows = losses[:rows] + loss_back
    image_grad = (scale * (image_parts[:rows] + image_back.astype(jnp.float32))).astype(jnp.bfloat16)
    text_grad = (scale * (text_sum[:rows] + text_back.astype(jnp.float32))).astype(jnp.bfloat16)
    return (loss_rows, image_grad, text_grad)


def solution(mesh):
    return jax.shard_map(
        per_device,
        mesh=mesh,
        in_specs=(
            P(("outer", "inner"), None),
            P(("outer", "inner"), None),
            P(("outer", "inner")),
            P(),
            P(),
        ),
        out_specs=(P(("outer", "inner")), P(("outer", "inner"), None), P(("outer", "inner"), None)),
        check_vma=False,
    )
```

```python
import jax
import jax.numpy as jnp
from jax import lax
from jax.experimental import pallas as pl
from jax.experimental.pallas import tpu as pltpu
from jax.sharding import PartitionSpec as P

IMAGE_PAIRS = [(0, 1), (1, 0), (2, 3), (3, 2)]
TEXT_PAIRS = [(1, 2), (2, 1), (3, 0), (0, 3)]

VMEM = pl.BlockSpec(memory_space=pltpu.VMEM)
SMEM = pl.BlockSpec(memory_space=pltpu.SMEM)
LIMIT = 40 * 1024 * 1024


def from_behind(block, distance):
    count = lax.axis_size("outer")
    return lax.ppermute(block, "outer", [((i - distance) % count, i) for i in range(count)])


def over_last(x, y):
    return lax.dot_general(x, y, (((1,), (1,)), ((), ())), preferred_element_type=jnp.float32)


def over_first(x, y):
    return lax.dot_general(x, y, (((0,), (0,)), ((), ())), preferred_element_type=jnp.float32)


def block_logits(texts, images, positive, first, scale, bias):
    logits = scale * over_last(texts, images) + bias
    row = lax.broadcasted_iota(jnp.int32, logits.shape, 0)
    return logits, row == positive - first


def block_weights(logits, hits):
    decay = jnp.exp(-jnp.abs(logits))
    share = 1.0 / (1.0 + decay)
    sigmoid = jnp.where(logits >= 0.0, share, decay * share)
    weights = (sigmoid - hits.astype(jnp.float32)).astype(jnp.bfloat16)
    return weights, decay


def block_loss(logits, hits, decay):
    signed = jnp.where(hits, -logits, logits)
    return jnp.sum(jnp.maximum(signed, 0.0) + jnp.log1p(decay), axis=0, keepdims=True)


def hold_kernel(images, texts, positive, images_out, texts_out, positive_out):
    images_out[...] = images[...]
    texts_out[...] = texts[...]
    positive_out[...] = positive[...]


def first_kernel(
    firsts, reals, image_0, image_1, text_0, text_1, prior, after, near, far, image_part, text_part, loss
):
    scale, bias = reals[0], reals[1]
    rows = image_0.shape[0]
    images, texts = (image_0, image_1), (text_0, text_1)
    for j in range(2):
        losses = jnp.zeros((1, rows), jnp.float32)
        total = None
        for k, text in enumerate((text_0, text_1, prior)):
            logits, hits = block_logits(
                text[...], images[j][...], near[pl.ds(j, 1), :], firsts[k], scale, bias
            )
            weights, decay = block_weights(logits, hits)
            losses += block_loss(logits, hits, decay)
            part = over_first(weights, text[...])
            total = part if total is None else total + part
            if k < 2:
                half = pl.ds(k * rows, rows)
                added = jnp.dot(weights, images[j][...], preferred_element_type=jnp.float32)
                text_part[half, :] = added if j == 0 else text_part[half, :] + added
        image_part[pl.ds(j * rows, rows), :] = total
        loss[pl.ds(j, 1), :] = losses
    for k in range(2):
        logits, hits = block_logits(texts[k][...], after[...], far[...], firsts[k], scale, bias)
        weights, _ = block_weights(logits, hits)
        text_part[pl.ds(k * rows, rows), :] += jnp.dot(
            weights, after[...], preferred_element_type=jnp.float32
        )


def image_kernel(
    firsts, reals, image_0, image_1, prior, near, image_part, loss, image_own, image_send, loss_own, loss_send
):
    scale, bias = reals[0], reals[1]
    rows = image_0.shape[0]
    for j, image in ((1, image_1), (0, image_0)):
        logits, hits = block_logits(
            prior[...], image[...], near[pl.ds(j, 1), :], firsts[3], scale, bias
        )
        weights, decay = block_weights(logits, hits)
        losses = loss[pl.ds(j, 1), :] + block_loss(logits, hits, decay)
        total = image_part[pl.ds(j * rows, rows), :] + over_first(weights, prior[...])
        if j == 1:
            image_send[...] = total.astype(jnp.bfloat16)
            loss_send[...] = losses
        else:
            image_own[...] = total
            loss_own[...] = losses


def text_kernel(firsts, reals, text_0, text_1, after, far, text_part, text_own, text_send):
    scale, bias = reals[0], reals[1]
    rows = text_0.shape[0]
    for k, text in ((1, text_1), (0, text_0)):
        logits, hits = block_logits(text[...], after[...], far[...], firsts[k], scale, bias)
        weights, _ = block_weights(logits, hits)
        total = text_part[pl.ds(k * rows, rows), :] + jnp.dot(
            weights, after[...], preferred_element_type=jnp.float32
        )
        if k == 1:
            text_send[...] = total.astype(jnp.bfloat16)
        else:
            text_own[...] = total


def call(kernel, name, in_specs, outs, blocks):
    return pl.pallas_call(
        kernel,
        name=name,
        out_shape=outs,
        in_specs=in_specs,
        out_specs=[VMEM] * len(outs),
        compiler_params=pltpu.CompilerParams(vmem_limit_bytes=LIMIT),
        cost_estimate=pl.CostEstimate(
            flops=2 * blocks * 256 * 256 * 1152, bytes_accessed=1 << 20, transcendentals=0
        ),
    )


def per_device(images, texts, positive, logit_scale, logit_bias):
    rows, width = texts.shape
    count = lax.axis_size("outer")
    group = lax.axis_index("outer")
    me = lax.axis_index("inner")
    whole = lax.axis_size("inner") * rows
    before = (group - 1 + count) % count
    firsts = jnp.stack(
        [
            group * whole + me * rows,
            group * whole + (3 - me) * rows,
            before * whole + me * rows,
            before * whole + (3 - me) * rows,
        ]
    ).astype(jnp.int32)
    reals = jnp.concatenate([logit_scale, logit_bias])
    shard = jax.ShapeDtypeStruct((rows, width), jnp.bfloat16)
    real_shard = jax.ShapeDtypeStruct((rows, width), jnp.float32)
    real_pair = jax.ShapeDtypeStruct((2 * rows, width), jnp.float32)
    line = jax.ShapeDtypeStruct((1, rows), jnp.float32)
    lines = jax.ShapeDtypeStruct((2, rows), jnp.float32)

    text_1 = lax.ppermute(texts, "inner", TEXT_PAIRS)
    image_1 = lax.ppermute(images, "inner", IMAGE_PAIRS)
    images_later, texts_later, mine = call(
        hold_kernel,
        "hold",
        [VMEM] * 3,
        [shard, shard, jax.ShapeDtypeStruct((1, rows), jnp.int32)],
        1,
    )(images, texts, positive[None, :])
    near = jnp.concatenate([mine, lax.ppermute(mine, "inner", IMAGE_PAIRS)])
    prior_0 = from_behind(texts_later, 1)
    after_0 = from_behind(images_later, -1)
    far = from_behind(near, -1)
    prior_1 = from_behind(text_1, 1)
    after_1 = from_behind(image_1, -1)

    image_part, text_part, loss = call(
        first_kernel, "first", [SMEM] * 2 + [VMEM] * 8, [real_pair, real_pair, lines], 20
    )(firsts, reals, images, image_1, texts, text_1, prior_0, after_0, near, far[:1])
    image_own, image_send, loss_own, loss_send = call(
        image_kernel, "image", [SMEM] * 2 + [VMEM] * 6, [real_shard, shard, line, line], 4
    )(firsts, reals, images, image_1, prior_1, near, image_part, loss)
    text_own, text_send = call(
        text_kernel, "text", [SMEM] * 2 + [VMEM] * 5, [real_shard, shard], 4
    )(firsts, reals, texts, text_1, after_1, far[1:], text_part)

    image_back = lax.ppermute(image_send, "inner", IMAGE_PAIRS)
    text_back = lax.ppermute(text_send, "inner", TEXT_PAIRS)
    loss_back = lax.ppermute(loss_send, "inner", IMAGE_PAIRS)
    scale = logit_scale[0]
    loss_rows = (loss_own + loss_back)[0]
    image_grad = (scale * (image_own + image_back.astype(jnp.float32))).astype(jnp.bfloat16)
    text_grad = (scale * (text_own + text_back.astype(jnp.float32))).astype(jnp.bfloat16)
    return (loss_rows, image_grad, text_grad)


def solution(mesh):
    return jax.shard_map(
        per_device,
        mesh=mesh,
        in_specs=(
            P(("outer", "inner"), None),
            P(("outer", "inner"), None),
            P(("outer", "inner")),
            P(),
            P(),
        ),
        out_specs=(P(("outer", "inner")), P(("outer", "inner"), None), P(("outer", "inner"), None)),
        check_vma=False,
    )
```

```python
import jax
import jax.numpy as jnp
from jax import lax
from jax.experimental import pallas as pl
from jax.experimental.pallas import tpu as pltpu
from jax.sharding import PartitionSpec as P

IMAGE_PAIRS = [(0, 1), (1, 0), (2, 3), (3, 2)]
TEXT_PAIRS = [(1, 2), (2, 1), (3, 0), (0, 3)]
PLANES = 3

SHIFTS = (0, 8, 16)
TAIL = 16

VMEM = pl.BlockSpec(memory_space=pltpu.VMEM)
SMEM = pl.BlockSpec(memory_space=pltpu.SMEM)
LIMIT = 40 * 1024 * 1024


def outer_pairs(distance, edge):
    count = lax.axis_size("outer")
    plane = count // PLANES
    pairs = [((i - distance) % count, i) for i in range(count)]
    return [(i, j) for i, j in pairs if (i // plane != j // plane) == edge]


def from_behind(block, distance):
    pairs = outer_pairs(distance, False) + outer_pairs(distance, True)
    return lax.ppermute(block, "outer", pairs)


def within_from_behind(block, distance):
    return lax.ppermute(block, "outer", outer_pairs(distance, False))


def over_last(x, y):
    return lax.dot_general(x, y, (((1,), (1,)), ((), ())), preferred_element_type=jnp.float32)


def over_first(x, y):
    return lax.dot_general(x, y, (((0,), (0,)), ((), ())), preferred_element_type=jnp.float32)


def hold_kernel(flags, images, texts, positive, images_out, texts_out, positive_out, edge_out):
    rows = images.shape[0]
    images_out[pl.ds(0, rows), :] = images[...]
    images_out[pl.ds(rows, TAIL), :] = jnp.zeros((TAIL, images.shape[1]), jnp.bfloat16)
    digits = [(positive[...] >> shift) & 255 for shift in SHIFTS]
    digits = jnp.concatenate(digits + [jnp.zeros((TAIL - len(SHIFTS), rows), jnp.int32)])
    images_out[pl.ds(rows, TAIL), pl.ds(0, rows)] = digits.astype(jnp.float32).astype(jnp.bfloat16)
    texts_out[...] = texts[...]
    positive_out[...] = positive[...]


    @pl.when(flags[1] == 1)
    def _():
        edge_out[pl.ds(0, rows), :] = texts[...]

    @pl.when(flags[1] == 0)
    def _():
        edge_out[...] = images_out[...]


def gate_kernel(*refs):
    pass


def gate(array, *tokens):
    anywhere = pl.BlockSpec(memory_space=pl.ANY)
    return pl.pallas_call(
        gate_kernel,
        name="gate",
        out_shape=jax.ShapeDtypeStruct(array.shape, array.dtype),
        in_specs=[anywhere] * (1 + len(tokens)),
        out_specs=anywhere,
        input_output_aliases={0: 0},
    )(array, *tokens)


class Blocks:
    def __init__(self, firsts, reals):
        self.firsts, self.scale, self.bias = firsts, reals[0], reals[1]

    def logits(self, text, image, positive, first):
        logits = self.scale * over_last(text, image) + self.bias
        row = lax.broadcasted_iota(jnp.int32, logits.shape, 0)
        return logits, row == positive - self.firsts[first]

    def __call__(self, text, image, positive, first):
        logits, hits = self.logits(text, image, positive, first)
        decay = jnp.exp(-jnp.abs(logits))
        share = 1.0 / (1.0 + decay)
        sigmoid = jnp.where(logits >= 0.0, share, decay * share)
        weights = (sigmoid - hits.astype(jnp.float32)).astype(jnp.bfloat16)

        def loss():
            signed = jnp.where(hits, -logits, logits)
            return jnp.sum(jnp.maximum(signed, 0.0) + jnp.log1p(decay), axis=0, keepdims=True)

        return weights, loss


def read_after(after):
    rows = after.shape[0] - TAIL
    digits = after[pl.ds(rows, TAIL), pl.ds(0, rows)].astype(jnp.float32).astype(jnp.int32)
    far = sum(digits[k : k + 1, :] << shift for k, shift in enumerate(SHIFTS))
    return after[pl.ds(0, rows), :], far


def by_image(weights, image):
    return jnp.dot(weights, image, preferred_element_type=jnp.float32)


def early_kernel(firsts, reals, images, texts, near, image_part, text_part, loss):
    block = Blocks(firsts, reals)
    weights, losses = block(texts[...], images[...], near[...], 0)
    loss[...] = losses()
    image_part[...] = over_first(weights, texts[...])
    text_part[...] = by_image(weights, images[...])


def first_kernel(
    firsts,
    reals,
    flags,
    image_0,
    image_1,
    text_0,
    text_1,
    prior,
    after,
    near,
    near_1,
    image_early,
    text_early,
    loss_early,
    image_part,
    text_part,
    loss,
):
    block = Blocks(firsts, reals)
    rows = image_0.shape[0]
    own, other = pl.ds(0, rows), pl.ds(rows, rows)

    weights, losses = block(text_1[...], image_0[...], near[...], 1)
    loss[pl.ds(0, 1), :] = loss_early[...] + losses()
    image_part[own, :] = image_early[...] + over_first(weights, text_1[...])
    text_part[other, :] = by_image(weights, image_0[...])

    weights, losses = block(text_0[...], image_1[...], near_1[...], 0)
    total = losses()
    image_part[other, :] = over_first(weights, text_0[...])
    text_part[own, :] = text_early[...] + by_image(weights, image_1[...])

    weights, losses = block(text_1[...], image_1[...], near_1[...], 1)
    loss[pl.ds(1, 1), :] = total + losses()
    image_part[other, :] += over_first(weights, text_1[...])
    text_part[other, :] += by_image(weights, image_1[...])

    @pl.when(flags[0] == 0)
    def _():
        for j, image, positive in ((0, image_0, near), (1, image_1, near_1)):
            weights, losses = block(prior[...], image[...], positive[...], 2)
            loss[pl.ds(j, 1), :] += losses()
            image_part[pl.ds(j * rows, rows), :] += over_first(weights, prior[...])

    @pl.when(flags[1] == 0)
    def _():
        image, far = read_after(after)
        for k, text in ((0, text_0), (1, text_1)):
            weights, _ = block(text[...], image, far, k)
            text_part[pl.ds(k * rows, rows), :] += by_image(weights, image)


def image_kernel(
    firsts,
    reals,
    flags,
    image_0,
    image_1,
    prior,
    edge,
    near,
    near_1,
    image_part,
    loss,
    image_own,
    image_send,
    loss_own,
    loss_send,
):
    block = Blocks(firsts, reals)
    rows = image_0.shape[0]
    for j, image, positive in ((1, image_1, near_1), (0, image_0, near)):
        part = pl.ds(j * rows, rows)
        weights, losses = block(prior[...], image[...], positive[...], 3)
        losses = loss[pl.ds(j, 1), :] + losses()
        total = image_part[part, :] + over_first(weights, prior[...])
        loss_out, image_out = (loss_send, image_send) if j == 1 else (loss_own, image_own)
        loss_out[...] = losses
        image_out[...] = total.astype(image_out.dtype)

        @pl.when(flags[0] == 1)
        def _():
            edge_text = edge[pl.ds(0, rows), :]
            weights, losses = block(prior[...], image[...], positive[...], 3)
            more, more_losses = block(edge_text, image[...], positive[...], 2)
            total = image_part[part, :] + over_first(weights, prior[...])
            total += over_first(more, edge_text)
            loss_out[...] = loss[pl.ds(j, 1), :] + losses() + more_losses()
            image_out[...] = total.astype(image_out.dtype)


def text_kernel(
    firsts, reals, flags, text_0, text_1, after, edge, far_1, text_part, text_own, text_send
):
    block = Blocks(firsts, reals)
    rows = text_0.shape[0]
    for k, text, text_out in ((1, text_1, text_send), (0, text_0, text_own)):
        part = pl.ds(k * rows, rows)
        weights, _ = block(text[...], after[...], far_1[...], k)
        total = text_part[part, :] + by_image(weights, after[...])
        text_out[...] = total.astype(text_out.dtype)

        @pl.when(flags[1] == 1)
        def _():
            weights, _ = block(text[...], after[...], far_1[...], k)
            edge_image, far = read_after(edge)
            more, _ = block(text[...], edge_image, far, k)
            total = text_part[part, :] + by_image(weights, after[...])
            text_out[...] = (total + by_image(more, edge_image)).astype(text_out.dtype)


def call(kernel, name, in_specs, outs, blocks):
    return pl.pallas_call(
        kernel,
        name=name,
        out_shape=outs,
        in_specs=in_specs,
        out_specs=[VMEM] * len(outs),
        compiler_params=pltpu.CompilerParams(vmem_limit_bytes=LIMIT),
        cost_estimate=pl.CostEstimate(
            flops=2 * blocks * 256 * 256 * 1152, bytes_accessed=1 << 20, transcendentals=0
        ),
    )


def per_device(images, texts, positive, logit_scale, logit_bias):
    rows, width = texts.shape
    count = lax.axis_size("outer")
    group = lax.axis_index("outer")
    me = lax.axis_index("inner")
    whole = lax.axis_size("inner") * rows
    before = (group - 1 + count) % count
    firsts = jnp.stack(
        [
            group * whole + me * rows,
            group * whole + (3 - me) * rows,
            before * whole + me * rows,
            before * whole + (3 - me) * rows,
        ]
    ).astype(jnp.int32)
    reals = jnp.concatenate([logit_scale, logit_bias])
    shard = jax.ShapeDtypeStruct((rows, width), jnp.bfloat16)
    long_shard = jax.ShapeDtypeStruct((rows + TAIL, width), jnp.bfloat16)
    real_shard = jax.ShapeDtypeStruct((rows, width), jnp.float32)
    real_pair = jax.ShapeDtypeStruct((2 * rows, width), jnp.float32)
    line = jax.ShapeDtypeStruct((1, rows), jnp.float32)
    lines = jax.ShapeDtypeStruct((2, rows), jnp.float32)

    plane = count // PLANES
    flags = jnp.stack([group % plane == 0, group % plane == plane - 1]).astype(jnp.int32)

    text_1 = lax.ppermute(texts, "inner", TEXT_PAIRS)
    image_1 = lax.ppermute(images, "inner", IMAGE_PAIRS)
    images_later, texts_later, near, edge_out = call(
        hold_kernel,
        "hold",
        [SMEM] + [VMEM] * 3,
        [long_shard, shard, jax.ShapeDtypeStruct((1, rows), jnp.int32), long_shard],
        1,
    )(flags, images, texts, positive[None, :])
    prior_0 = within_from_behind(texts_later, 1)
    after_0 = within_from_behind(images_later, -1)
    image_early, text_early, loss_early = call(
        early_kernel, "early", [SMEM] * 2 + [VMEM] * 3, [real_shard, real_shard, line], 3
    )(firsts, reals, images, texts, near)
    near_1 = lax.ppermute(positive[None, :], "inner", IMAGE_PAIRS)
    image_1 = gate(image_1, near_1, loss_early)
    after_1 = from_behind(image_1, -1)
    text_1 = gate(text_1, near_1, loss_early)
    prior_1 = from_behind(text_1, 1)
    far_1 = from_behind(near_1, -1)
    edge = lax.ppermute(gate(edge_out, text_1, image_1), "outer", outer_pairs(1, True) + outer_pairs(-1, True))

    image_part, text_part, loss = call(
        first_kernel, "first", [SMEM] * 3 + [VMEM] * 11, [real_pair, real_pair, lines], 17
    )(
        firsts,
        reals,
        flags,
        images,
        image_1,
        texts,
        text_1,
        prior_0,
        after_0,
        near,
        near_1,
        image_early,
        text_early,
        loss_early,
    )
    text_own, text_send = call(
        text_kernel, "text", [SMEM] * 3 + [VMEM] * 6, [real_shard, shard], 4
    )(firsts, reals, flags, texts, text_1, after_1, edge, far_1, text_part)
    image_own, image_send, loss_own, loss_send = call(
        image_kernel, "image", [SMEM] * 3 + [VMEM] * 8, [real_shard, shard, line, line], 4
    )(firsts, reals, flags, images, image_1, prior_1, edge, near, near_1, image_part, loss)

    image_back = lax.ppermute(image_send, "inner", IMAGE_PAIRS)
    text_back = lax.ppermute(text_send, "inner", TEXT_PAIRS)
    loss_back = lax.ppermute(loss_send, "inner", IMAGE_PAIRS)
    scale = logit_scale[0]
    loss_rows = (loss_own + loss_back)[0]
    image_grad = (scale * (image_own + image_back.astype(jnp.float32))).astype(jnp.bfloat16)
    text_grad = (scale * (text_own + text_back.astype(jnp.float32))).astype(jnp.bfloat16)
    return (loss_rows, image_grad, text_grad)


def solution(mesh):
    return jax.shard_map(
        per_device,
        mesh=mesh,
        in_specs=(
            P(("outer", "inner"), None),
            P(("outer", "inner"), None),
            P(("outer", "inner")),
            P(),
            P(),
        ),
        out_specs=(P(("outer", "inner")), P(("outer", "inner"), None), P(("outer", "inner"), None)),
        check_vma=False,
    )
```

```python
import jax
import jax.numpy as jnp
from jax import lax
from jax.experimental import pallas as pl
from jax.experimental.pallas import tpu as pltpu
from jax.sharding import PartitionSpec as P

IMAGE_PAIRS = [(0, 1), (1, 0), (2, 3), (3, 2)]
TEXT_PAIRS = [(1, 2), (2, 1), (3, 0), (0, 3)]

SHIFTS = (0, 8, 16)
TAIL = 16

VMEM = pl.BlockSpec(memory_space=pltpu.VMEM)
SMEM = pl.BlockSpec(memory_space=pltpu.SMEM)
LIMIT = 40 * 1024 * 1024


def from_behind(block, distance):
    count = lax.axis_size("outer")
    return lax.ppermute(block, "outer", [((i - distance) % count, i) for i in range(count)])


def over_last(x, y):
    return lax.dot_general(x, y, (((1,), (1,)), ((), ())), preferred_element_type=jnp.float32)


def over_first(x, y):
    return lax.dot_general(x, y, (((0,), (0,)), ((), ())), preferred_element_type=jnp.float32)


def hold_kernel(images, texts, positive, images_out, texts_out):
    rows = images.shape[0]
    images_out[pl.ds(0, rows), :] = images[...]
    images_out[pl.ds(rows, TAIL), :] = jnp.zeros((TAIL, images.shape[1]), jnp.bfloat16)
    digits = [(positive[...] >> shift) & 255 for shift in SHIFTS]
    digits = jnp.concatenate(digits + [jnp.zeros((TAIL - len(SHIFTS), rows), jnp.int32)])
    images_out[pl.ds(rows, TAIL), pl.ds(0, rows)] = digits.astype(jnp.float32).astype(jnp.bfloat16)
    texts_out[...] = texts[...]


class Blocks:
    def __init__(self, firsts, reals):
        self.firsts, self.scale, self.bias = firsts, reals[0], reals[1]

    def logits(self, text, image, positive, first):
        logits = self.scale * over_last(text, image) + self.bias
        row = lax.broadcasted_iota(jnp.int32, logits.shape, 0)
        return logits, row == positive - self.firsts[first]

    def __call__(self, text, image, positive, first):
        logits, hits = self.logits(text, image, positive, first)
        decay = jnp.exp(-jnp.abs(logits))
        share = 1.0 / (1.0 + decay)
        sigmoid = jnp.where(logits >= 0.0, share, decay * share)
        weights = (sigmoid - hits.astype(jnp.float32)).astype(jnp.bfloat16)

        def loss():
            signed = jnp.where(hits, -logits, logits)
            return jnp.sum(jnp.maximum(signed, 0.0) + jnp.log1p(decay), axis=0, keepdims=True)

        return weights, loss


def read_after(after):
    rows = after.shape[0] - TAIL
    digits = after[pl.ds(rows, TAIL), pl.ds(0, rows)].astype(jnp.float32).astype(jnp.int32)
    far = sum(digits[k : k + 1, :] << shift for k, shift in enumerate(SHIFTS))
    return after[pl.ds(0, rows), :], far


def by_image(weights, image):
    return jnp.dot(weights, image, preferred_element_type=jnp.float32)


def gate_kernel(*refs):
    pass


def gate(array, *tokens):
    anywhere = pl.BlockSpec(memory_space=pl.ANY)
    return pl.pallas_call(
        gate_kernel,
        name="gate",
        out_shape=pltpu.VMEM(array.shape, array.dtype),
        in_specs=[anywhere] * (1 + len(tokens)),
        out_specs=anywhere,
        input_output_aliases={0: 0},
    )(pltpu.with_memory_space_constraint(array, pltpu.VMEM), *tokens)


def first_kernel(
    firsts,
    reals,
    image_0,
    image_1,
    text_0,
    text_1,
    prior_0,
    after_0,
    near_0,
    near_1,
    image_part,
    text_part,
    loss_part,
):
    block = Blocks(firsts, reals)
    weights, losses = block(text_1[...], image_1[...], near_1[...], 1)
    image_part[...] = over_first(weights, text_1[...])
    text_part[...] = by_image(weights, image_1[...])
    loss_part[...] = losses()
    weights, losses = block(text_0[...], image_1[...], near_1[...], 0)
    image_part[...] += over_first(weights, text_0[...])
    loss_part[...] += losses()
    weights, losses = block(prior_0[...], image_1[...], near_1[...], 2)
    image_part[...] += over_first(weights, prior_0[...])
    loss_part[...] += losses()
    weights, _ = block(text_1[...], image_0[...], near_0[...], 1)
    text_part[...] += by_image(weights, image_0[...])
    image, far = read_after(after_0)
    weights, _ = block(text_1[...], image, far, 1)
    text_part[...] += by_image(weights, image)


def text_kernel(firsts, reals, text_1, after_1, far_1, text_part, text_send):
    weights, _ = Blocks(firsts, reals)(text_1[...], after_1[...], far_1[...], 1)
    total = text_part[...] + by_image(weights, after_1[...])
    text_send[...] = total.astype(text_send.dtype)


def image_kernel(
    firsts, reals, image_1, prior_1, near_1, image_part, loss_part, sent, image_send, loss_send
):
    weights, losses = Blocks(firsts, reals)(prior_1[...], image_1[...], near_1[...], 3)
    total = image_part[...] + over_first(weights, prior_1[...])
    image_send[...] = total.astype(image_send.dtype)
    loss_send[...] = loss_part[...] + losses()


def late_kernel(
    firsts,
    reals,
    image_0,
    image_1,
    text_0,
    text_1,
    prior_0,
    prior_1,
    after_0,
    after_1,
    near_0,
    near_1,
    far_1,
    image_sent,
    image_own,
    text_own,
    loss_own,
):
    block = Blocks(firsts, reals)
    weights, losses = block(text_0[...], image_0[...], near_0[...], 0)
    image_own[...] = over_first(weights, text_0[...])
    text_own[...] = by_image(weights, image_0[...])
    loss_own[...] = losses()
    for k, text in ((1, text_1), (2, prior_0), (3, prior_1)):
        weights, losses = block(text[...], image_0[...], near_0[...], k)
        image_own[...] += over_first(weights, text[...])
        loss_own[...] += losses()
    after, far = read_after(after_0)
    for image, positive in ((image_1[...], near_1[...]), (after, far), (after_1[...], far_1[...])):
        weights, _ = block(text_0[...], image, positive, 0)
        text_own[...] += by_image(weights, image)


def call(kernel, name, in_specs, outs, blocks):
    return pl.pallas_call(
        kernel,
        name=name,
        out_shape=outs,
        in_specs=in_specs,
        out_specs=[VMEM] * len(outs),
        compiler_params=pltpu.CompilerParams(vmem_limit_bytes=LIMIT),
        cost_estimate=pl.CostEstimate(
            flops=2 * blocks * 256 * 256 * 1152, bytes_accessed=1 << 20, transcendentals=0
        ),
    )


def per_device(images, texts, positive, logit_scale, logit_bias):
    rows, width = texts.shape
    count = lax.axis_size("outer")
    group = lax.axis_index("outer")
    me = lax.axis_index("inner")
    whole = lax.axis_size("inner") * rows
    before = (group - 1 + count) % count
    firsts = jnp.stack(
        [
            group * whole + me * rows,
            group * whole + (3 - me) * rows,
            before * whole + me * rows,
            before * whole + (3 - me) * rows,
        ]
    ).astype(jnp.int32)
    reals = jnp.concatenate([logit_scale, logit_bias])
    shard = jax.ShapeDtypeStruct((rows, width), jnp.bfloat16)
    long_shard = jax.ShapeDtypeStruct((rows + TAIL, width), jnp.bfloat16)
    real_shard = jax.ShapeDtypeStruct((rows, width), jnp.float32)
    line = jax.ShapeDtypeStruct((1, rows), jnp.float32)

    text_1 = lax.ppermute(texts, "inner", TEXT_PAIRS)
    image_1 = lax.ppermute(images, "inner", IMAGE_PAIRS)
    near_0 = positive[None, :]
    images_later, texts_later = call(
        hold_kernel, "hold", [VMEM] * 3, [long_shard, shard], 1
    )(images, texts, near_0)
    near_1 = lax.ppermute(near_0, "inner", IMAGE_PAIRS)
    prior_0 = from_behind(texts_later, 1)
    after_0 = from_behind(images_later, -1)
    image_1 = gate(image_1, near_1)
    after_1 = from_behind(image_1, -1)
    prior_1 = from_behind(text_1, 1)
    far_1 = from_behind(near_1, -1)

    image_part, text_part, loss_part = call(
        first_kernel, "first", [SMEM] * 2 + [VMEM] * 8, [real_shard, real_shard, line], 11
    )(firsts, reals, images, image_1, texts, text_1, prior_0, after_0, near_0, near_1)
    (text_send,) = call(text_kernel, "text", [SMEM] * 2 + [VMEM] * 4, [shard], 2)(
        firsts, reals, text_1, after_1, far_1, text_part
    )
    image_send, loss_send = call(image_kernel, "image", [SMEM] * 2 + [VMEM] * 5 + [pl.BlockSpec(memory_space=pl.ANY)], [shard, line], 2)(
        firsts, reals, image_1, prior_1, near_1, image_part, loss_part, text_send
    )
    image_own, text_own, loss_own = call(
        late_kernel,
        "late",
        [SMEM] * 2 + [VMEM] * 11 + [pl.BlockSpec(memory_space=pl.ANY)],
        [real_shard, real_shard, line],
        15,
    )(
        firsts,
        reals,
        images,
        image_1,
        texts,
        text_1,
        prior_0,
        prior_1,
        after_0,
        after_1,
        near_0,
        near_1,
        far_1,
        image_send,
    )
    image_back = lax.ppermute(image_send, "inner", IMAGE_PAIRS)
    text_back = lax.ppermute(text_send, "inner", TEXT_PAIRS)
    loss_back = lax.ppermute(loss_send, "inner", IMAGE_PAIRS)
    scale = logit_scale[0]
    loss_rows = (loss_own + loss_back)[0]
    image_grad = (scale * (image_own + image_back.astype(jnp.float32))).astype(jnp.bfloat16)
    text_grad = (scale * (text_own + text_back.astype(jnp.float32))).astype(jnp.bfloat16)
    return (loss_rows, image_grad, text_grad)


def solution(mesh):
    return jax.shard_map(
        per_device,
        mesh=mesh,
        in_specs=(
            P(("outer", "inner"), None),
            P(("outer", "inner"), None),
            P(("outer", "inner")),
            P(),
            P(),
        ),
        out_specs=(P(("outer", "inner")), P(("outer", "inner"), None), P(("outer", "inner"), None)),
        check_vma=False,
    )
```

```python
import jax
import jax.numpy as jnp
from jax import lax
from jax.experimental import pallas as pl
from jax.experimental.pallas import tpu as pltpu
from jax.sharding import PartitionSpec as P

IMAGE_PAIRS = [(0, 1), (1, 0), (2, 3), (3, 2)]
TEXT_PAIRS = [(1, 2), (2, 1), (3, 0), (0, 3)]

SHIFTS = (0, 8, 16)
TAIL = 16

VMEM = pl.BlockSpec(memory_space=pltpu.VMEM)
SMEM = pl.BlockSpec(memory_space=pltpu.SMEM)
LIMIT = 40 * 1024 * 1024
GATE_BLOCKS = 120


def from_behind(block, distance):
    count = lax.axis_size("outer")
    return lax.ppermute(block, "outer", [((i - distance) % count, i) for i in range(count)])


def over_last(x, y):
    return lax.dot_general(x, y, (((1,), (1,)), ((), ())), preferred_element_type=jnp.float32)


def over_first(x, y):
    return lax.dot_general(x, y, (((0,), (0,)), ((), ())), preferred_element_type=jnp.float32)


def hold_kernel(places, scale, bias, images, texts, near_0, near_1, images_out, texts_out):
    rows = images.shape[0]
    images_out[pl.ds(0, rows), :] = images[...]
    images_out[pl.ds(rows, TAIL), :] = jnp.zeros((TAIL, images.shape[1]), jnp.bfloat16)
    digits = [(near[...] >> shift) & 255 for near in (near_0, near_1) for shift in SHIFTS]
    digits = jnp.concatenate(digits + [jnp.zeros((TAIL - len(digits), rows), jnp.int32)])
    images_out[pl.ds(rows, TAIL), pl.ds(0, rows)] = digits.astype(jnp.float32).astype(jnp.bfloat16)
    texts_out[...] = texts[...]


class Blocks:
    def __init__(self, places, scale, bias):
        self.firsts, self.scale, self.bias = places, scale[0], bias[0]

    def logits(self, text, image, positive, first):
        logits = self.scale * over_last(text, image) + self.bias
        row = lax.broadcasted_iota(jnp.int32, logits.shape, 0)
        return logits, row == positive - self.firsts[first]

    def __call__(self, text, image, positive, first):
        logits, hits = self.logits(text, image, positive, first)
        decay = jnp.exp(-jnp.abs(logits))
        share = 1.0 / (1.0 + decay)
        sigmoid = jnp.where(logits >= 0.0, share, decay * share)
        weights = (sigmoid - hits.astype(jnp.float32)).astype(jnp.bfloat16)

        def loss():
            signed = jnp.where(hits, -logits, logits)
            return jnp.sum(jnp.maximum(signed, 0.0) + jnp.log1p(decay), axis=0, keepdims=True)

        return weights, loss


def read_far(after, shard):
    rows = after.shape[0] - TAIL
    digits = after[pl.ds(rows, TAIL), pl.ds(0, rows)].astype(jnp.float32).astype(jnp.int32)
    first = shard * len(SHIFTS)
    return sum(digits[first + k : first + k + 1, :] << shift for k, shift in enumerate(SHIFTS))


def by_image(weights, image):
    return jnp.dot(weights, image, preferred_element_type=jnp.float32)


def gate_kernel(*refs):
    pass


def gate(array, *tokens):
    anywhere = pl.BlockSpec(memory_space=pl.ANY)
    return pl.pallas_call(
        gate_kernel,
        name="gate",
        out_shape=pltpu.VMEM(array.shape, array.dtype),
        in_specs=[anywhere] * (1 + len(tokens)),
        out_specs=anywhere,
        input_output_aliases={0: 0},
        cost_estimate=cost(GATE_BLOCKS),
    )(pltpu.with_memory_space_constraint(array, pltpu.VMEM), *tokens)


def first_kernel(
    places,
    scale,
    bias,
    image_0,
    image_1,
    text_0,
    text_1,
    prior_0,
    after_0,
    near_0,
    near_1,
    image_part,
    text_part,
    loss_part,
):
    block = Blocks(places, scale, bias)
    weights, losses = block(text_1[...], image_1[...], near_1[...], 1)
    image_part[...] = over_first(weights, text_1[...])
    text_part[...] = by_image(weights, image_1[...])
    loss_part[...] = losses()
    weights, losses = block(text_0[...], image_1[...], near_1[...], 0)
    image_part[...] += over_first(weights, text_0[...])
    loss_part[...] += losses()
    weights, losses = block(prior_0[...], image_1[...], near_1[...], 2)
    image_part[...] += over_first(weights, prior_0[...])
    loss_part[...] += losses()
    weights, _ = block(text_1[...], image_0[...], near_0[...], 1)
    text_part[...] += by_image(weights, image_0[...])
    after = after_0[pl.ds(0, image_0.shape[0]), :]
    weights, _ = block(text_1[...], after, read_far(after_0, 0), 1)
    text_part[...] += by_image(weights, after)


def text_kernel(places, scale, bias, text_1, after_0, after_1, text_part, sent, text_send):
    weights, _ = Blocks(places, scale, bias)(text_1[...], after_1[...], read_far(after_0, 1), 1)
    total = text_part[...] + by_image(weights, after_1[...])
    text_send[...] = total.astype(text_send.dtype)


def image_kernel(
    places,
    scale,
    bias,
    image_1,
    prior_1,
    near_1,
    image_part,
    loss_part,
    image_send,
    loss_send,
):
    weights, losses = Blocks(places, scale, bias)(prior_1[...], image_1[...], near_1[...], 3)
    total = image_part[...] + over_first(weights, prior_1[...])
    image_send[...] = total.astype(image_send.dtype)
    loss_send[...] = loss_part[...] + losses()


def late_kernel(
    places,
    scale,
    bias,
    image_0,
    image_1,
    text_0,
    text_1,
    prior_0,
    prior_1,
    after_0,
    after_1,
    near_0,
    near_1,
    sent,
    image_own,
    text_own,
    loss_own,
):
    block = Blocks(places, scale, bias)
    weights, losses = block(text_0[...], image_0[...], near_0[...], 0)
    image_own[...] = over_first(weights, text_0[...])
    text_own[...] = by_image(weights, image_0[...])
    loss_own[...] = losses()
    for k, text in ((1, text_1), (2, prior_0), (3, prior_1)):
        weights, losses = block(text[...], image_0[...], near_0[...], k)
        image_own[...] += over_first(weights, text[...])
        loss_own[...] += losses()
    after = after_0[pl.ds(0, image_0.shape[0]), :]
    for image, positive in (
        (image_1[...], near_1[...]),
        (after, read_far(after_0, 0)),
        (after_1[...], read_far(after_0, 1)),
    ):
        weights, _ = block(text_0[...], image, positive, 0)
        text_own[...] += by_image(weights, image)


def cost(blocks):
    return pl.CostEstimate(
        flops=2 * blocks * 256 * 256 * 1152, bytes_accessed=1 << 20, transcendentals=0
    )


def call(kernel, name, in_specs, outs, blocks):
    return pl.pallas_call(
        kernel,
        name=name,
        out_shape=outs,
        in_specs=in_specs,
        out_specs=[VMEM] * len(outs),
        compiler_params=pltpu.CompilerParams(vmem_limit_bytes=LIMIT),
        cost_estimate=cost(blocks),
    )


def per_device(images, texts, positive, logit_scale, logit_bias):
    rows, width = texts.shape
    count = lax.axis_size("outer")
    group = lax.axis_index("outer")
    me = lax.axis_index("inner")
    whole = lax.axis_size("inner") * rows
    before = (group - 1 + count) % count
    places = jnp.stack(
        [
            group * whole + me * rows,
            group * whole + (3 - me) * rows,
            before * whole + me * rows,
            before * whole + (3 - me) * rows,
        ]
    ).astype(jnp.int32)
    scalars = (places, logit_scale, logit_bias)
    shard = jax.ShapeDtypeStruct((rows, width), jnp.bfloat16)
    long_shard = jax.ShapeDtypeStruct((rows + TAIL, width), jnp.bfloat16)
    real_shard = jax.ShapeDtypeStruct((rows, width), jnp.float32)
    line = jax.ShapeDtypeStruct((1, rows), jnp.float32)
    anywhere = [pl.BlockSpec(memory_space=pl.ANY)]

    near_0 = positive[None, :]
    near_1 = lax.ppermute(near_0, "inner", IMAGE_PAIRS)
    text_1 = gate(lax.ppermute(texts, "inner", TEXT_PAIRS))
    image_1 = gate(lax.ppermute(images, "inner", IMAGE_PAIRS))
    images_later, texts_later = call(
        hold_kernel, "hold", [SMEM] * 3 + [VMEM] * 4, [long_shard, shard], 1
    )(*scalars, images, texts, near_0, near_1)
    prior_0 = from_behind(texts_later, 1)
    after_0 = from_behind(images_later, -1)
    after_1 = from_behind(image_1, -1)
    prior_1 = from_behind(text_1, 1)

    image_part, text_part, loss_part = call(
        first_kernel, "first", [SMEM] * 3 + [VMEM] * 8, [real_shard, real_shard, line], 11
    )(*scalars, images, image_1, texts, text_1, prior_0, after_0, near_0, near_1)
    image_send, loss_send = call(
        image_kernel, "image", [SMEM] * 3 + [VMEM] * 5, [shard, line], 2
    )(*scalars, image_1, prior_1, near_1, image_part, loss_part)
    (text_send,) = call(text_kernel, "text", [SMEM] * 3 + [VMEM] * 4 + anywhere, [shard], 2)(
        *scalars, text_1, after_0, after_1, text_part, image_send
    )
    image_own, text_own, loss_own = call(
        late_kernel,
        "late",
        [SMEM] * 3 + [VMEM] * 10 + anywhere,
        [real_shard, real_shard, line],
        15,
    )(
        *scalars,
        images,
        image_1,
        texts,
        text_1,
        prior_0,
        prior_1,
        after_0,
        after_1,
        near_0,
        near_1,
        text_send,
    )

    image_back = lax.ppermute(image_send, "inner", IMAGE_PAIRS)
    text_back = lax.ppermute(text_send, "inner", TEXT_PAIRS)
    loss_back = lax.ppermute(loss_send, "inner", IMAGE_PAIRS)
    scale = logit_scale[0]
    loss_rows = (loss_own + loss_back)[0]
    image_grad = (scale * (image_own + image_back.astype(jnp.float32))).astype(jnp.bfloat16)
    text_grad = (scale * (text_own + text_back.astype(jnp.float32))).astype(jnp.bfloat16)
    return (loss_rows, image_grad, text_grad)


def solution(mesh):
    return jax.shard_map(
        per_device,
        mesh=mesh,
        in_specs=(
            P(("outer", "inner"), None),
            P(("outer", "inner"), None),
            P(("outer", "inner")),
            P(),
            P(),
        ),
        out_specs=(P(("outer", "inner")), P(("outer", "inner"), None), P(("outer", "inner"), None)),
        check_vma=False,
    )
```

```python
import jax
import jax.numpy as jnp
from jax import lax
from jax.experimental import pallas as pl
from jax.experimental.pallas import tpu as pltpu
from jax.sharding import PartitionSpec as P

IMAGE_PAIRS = [(0, 1), (1, 0), (2, 3), (3, 2)]
TEXT_PAIRS = [(1, 2), (2, 1), (3, 0), (0, 3)]

SHIFTS = (0, 8, 16)
TAIL = 16

VMEM = pl.BlockSpec(memory_space=pltpu.VMEM)
SMEM = pl.BlockSpec(memory_space=pltpu.SMEM)
LIMIT = 40 * 1024 * 1024
ROOM = 5
IS_FIRST, IS_LAST = 4, 5


PLANES = 3


def from_behind(block, distance, within=False):
    count = lax.axis_size("outer")
    plane = count // PLANES
    pairs = [((i - distance) % count, i) for i in range(count)]
    if within:
        pairs = [(i, j) for i, j in pairs if i // plane == j // plane]
    return lax.ppermute(block, "outer", pairs)


def over_edge(block):
    plane = lax.axis_size("outer") // PLANES
    pairs = [(k * plane + plane - 1, (k + 1) % PLANES * plane) for k in range(PLANES)]
    return lax.ppermute(block, "outer", pairs + [(j, i) for i, j in pairs])


def over_last(x, y):
    return lax.dot_general(x, y, (((1,), (1,)), ((), ())), preferred_element_type=jnp.float32)


def over_first(x, y):
    return lax.dot_general(x, y, (((0,), (0,)), ((), ())), preferred_element_type=jnp.float32)


def hold_kernel(
    places, scale, bias, images, texts, positive, images_out, texts_out, edge_out
):
    rows = images.shape[0]
    images_out[pl.ds(0, rows), :] = images[...]
    images_out[pl.ds(rows, TAIL), :] = jnp.zeros((TAIL, images.shape[1]), jnp.bfloat16)
    digits = [(positive[...] >> shift) & 255 for shift in SHIFTS]
    digits = jnp.concatenate(digits + [jnp.zeros((TAIL - len(SHIFTS), rows), jnp.int32)])
    images_out[pl.ds(rows, TAIL), pl.ds(0, rows)] = digits.astype(jnp.float32).astype(jnp.bfloat16)
    texts_out[...] = texts[...]

    @pl.when(places[IS_LAST] == 1)
    def _():
        edge_out[pl.ds(0, rows), :] = texts[...]

    @pl.when(places[IS_LAST] == 0)
    def _():
        edge_out[...] = images_out[...]


class Blocks:
    def __init__(self, places, scale, bias):
        self.firsts, self.scale, self.bias = places, scale[0], bias[0]

    def logits(self, text, image, positive, first):
        logits = self.scale * over_last(text, image) + self.bias
        row = lax.broadcasted_iota(jnp.int32, logits.shape, 0)
        return logits, row == positive - self.firsts[first]

    def __call__(self, text, image, positive, first):
        logits, hits = self.logits(text, image, positive, first)
        decay = jnp.exp(-jnp.abs(logits))
        share = 1.0 / (1.0 + decay)
        sigmoid = jnp.where(logits >= 0.0, share, decay * share)
        weights = (sigmoid - hits.astype(jnp.float32)).astype(jnp.bfloat16)

        def loss():
            signed = jnp.where(hits, -logits, logits)
            return jnp.sum(jnp.maximum(signed, 0.0) + jnp.log1p(decay), axis=0, keepdims=True)

        return weights, loss


def read_after(after):
    rows = after.shape[0] - TAIL
    digits = after[pl.ds(rows, TAIL), pl.ds(0, rows)].astype(jnp.float32).astype(jnp.int32)
    far = sum(digits[k : k + 1, :] << shift for k, shift in enumerate(SHIFTS))
    return after[pl.ds(0, rows), :], far


def by_image(weights, image):
    return jnp.dot(weights, image, preferred_element_type=jnp.float32)


def gate_kernel(*refs):
    pass


def gate(array, *tokens, blocks=0):
    anywhere = pl.BlockSpec(memory_space=pl.ANY)
    return pl.pallas_call(
        gate_kernel,
        name="gate",
        out_shape=pltpu.VMEM(array.shape, array.dtype),
        in_specs=[anywhere] * (1 + len(tokens)),
        out_specs=anywhere,
        input_output_aliases={0: 0},
        cost_estimate=cost(blocks),
    )(pltpu.with_memory_space_constraint(array, pltpu.VMEM), *tokens)


def first_kernel(
    places,
    scale,
    bias,
    image_0,
    image_1,
    text_0,
    text_1,
    prior_0,
    after_0,
    near_0,
    near_1,
    image_part,
    text_part,
    loss_part,
    near_out,
):
    near_out[...] = near_1[...]
    block = Blocks(places, scale, bias)
    weights, losses = block(text_1[...], image_1[...], near_1[...], 1)
    image_part[...] = over_first(weights, text_1[...])
    text_part[...] = by_image(weights, image_1[...])
    loss_part[...] = losses()
    weights, losses = block(text_0[...], image_1[...], near_1[...], 0)
    image_part[...] += over_first(weights, text_0[...])
    loss_part[...] += losses()
    weights, _ = block(text_1[...], image_0[...], near_0[...], 1)
    text_part[...] += by_image(weights, image_0[...])

    @pl.when(places[IS_FIRST] == 0)
    def _():
        weights, losses = block(prior_0[...], image_1[...], near_1[...], 2)
        image_part[...] += over_first(weights, prior_0[...])
        loss_part[...] += losses()

    @pl.when(places[IS_LAST] == 0)
    def _():
        image, far = read_after(after_0)
        weights, _ = block(text_1[...], image, far, 1)
        text_part[...] += by_image(weights, image)


def image_kernel(
    places,
    scale,
    bias,
    image_1,
    prior_1,
    near_1,
    image_part,
    loss_part,
    edge,
    image_send,
    loss_send,
):
    block = Blocks(places, scale, bias)
    weights, losses = block(prior_1[...], image_1[...], near_1[...], 3)
    total = image_part[...] + over_first(weights, prior_1[...])
    loss_send[...] = loss_part[...] + losses()
    image_send[...] = total.astype(image_send.dtype)

    @pl.when(places[IS_FIRST] == 1)
    def _():
        prior_0 = edge[pl.ds(0, image_1.shape[0]), :]
        weights, _ = block(prior_1[...], image_1[...], near_1[...], 3)
        more, losses = block(prior_0, image_1[...], near_1[...], 2)
        total = image_part[...] + over_first(weights, prior_1[...]) + over_first(more, prior_0)
        loss_send[...] += losses()
        image_send[...] = total.astype(image_send.dtype)


def text_kernel(
    places,
    scale,
    bias,
    text_1,
    after_1,
    far_1,
    text_part,
    edge,
    sent,
    text_send,
):
    block = Blocks(places, scale, bias)
    weights, _ = block(text_1[...], after_1[...], far_1[...], 1)
    total = text_part[...] + by_image(weights, after_1[...])
    text_send[...] = total.astype(text_send.dtype)

    @pl.when(places[IS_LAST] == 1)
    def _():
        after_0, far_0 = read_after(edge)
        weights, _ = block(text_1[...], after_1[...], far_1[...], 1)
        more, _ = block(text_1[...], after_0, far_0, 1)
        total = text_part[...] + by_image(weights, after_1[...]) + by_image(more, after_0)
        text_send[...] = total.astype(text_send.dtype)


def late_kernel(
    places,
    scale,
    bias,
    image_0,
    image_1,
    text_0,
    text_1,
    prior_0,
    prior_1,
    after_0,
    after_1,
    near_0,
    near_1,
    far_1,
    edge,
    sent,
    image_own,
    text_own,
    loss_own,
):
    block = Blocks(places, scale, bias)
    rows = image_0.shape[0]
    weights, losses = block(text_0[...], image_0[...], near_0[...], 0)
    image_own[...] = over_first(weights, text_0[...])
    text_own[...] = by_image(weights, image_0[...])
    loss_own[...] = losses()

    def add_image(text, k):
        weights, losses = block(text, image_0[...], near_0[...], k)
        image_own[...] += over_first(weights, text)
        loss_own[...] += losses()

    def add_text(image, positive):
        weights, _ = block(text_0[...], image, positive, 0)
        text_own[...] += by_image(weights, image)

    add_image(text_1[...], 1)
    add_image(prior_1[...], 3)
    add_text(image_1[...], near_1[...])
    add_text(after_1[...], far_1[...])

    @pl.when(places[IS_FIRST] == 0)
    def _():
        add_image(prior_0[...], 2)

    @pl.when(places[IS_FIRST] == 1)
    def _():
        add_image(edge[pl.ds(0, rows), :], 2)

    @pl.when(places[IS_LAST] == 0)
    def _():
        add_text(*read_after(after_0))

    @pl.when(places[IS_LAST] == 1)
    def _():
        add_text(*read_after(edge))


def cost(blocks):
    return pl.CostEstimate(
        flops=2 * blocks * 256 * 256 * 1152, bytes_accessed=1 << 20, transcendentals=0
    )


def call(kernel, name, in_specs, outs, blocks):
    return pl.pallas_call(
        kernel,
        name=name,
        out_shape=outs,
        in_specs=in_specs,
        out_specs=[VMEM] * len(outs),
        compiler_params=pltpu.CompilerParams(vmem_limit_bytes=LIMIT),
        cost_estimate=cost(blocks),
    )


def per_device(images, texts, positive, logit_scale, logit_bias):
    rows, width = texts.shape
    count = lax.axis_size("outer")
    group = lax.axis_index("outer")
    me = lax.axis_index("inner")
    whole = lax.axis_size("inner") * rows
    before = (group - 1 + count) % count
    plane = count // PLANES
    places = jnp.stack(
        [
            group * whole + me * rows,
            group * whole + (3 - me) * rows,
            before * whole + me * rows,
            before * whole + (3 - me) * rows,
            (group % plane == 0).astype(jnp.int32),
            (group % plane == plane - 1).astype(jnp.int32),
        ]
    ).astype(jnp.int32)
    scalars = (places, logit_scale, logit_bias)
    shard = jax.ShapeDtypeStruct((rows, width), jnp.bfloat16)
    long_shard = jax.ShapeDtypeStruct((rows + TAIL, width), jnp.bfloat16)
    real_shard = jax.ShapeDtypeStruct((rows, width), jnp.float32)
    line = jax.ShapeDtypeStruct((1, rows), jnp.float32)
    int_line = jax.ShapeDtypeStruct((1, rows), jnp.int32)
    anywhere = [pl.BlockSpec(memory_space=pl.ANY)]

    text_1 = lax.ppermute(texts, "inner", TEXT_PAIRS)
    image_1 = lax.ppermute(images, "inner", IMAGE_PAIRS)
    near_0 = positive[None, :]
    images_later, texts_later, edge = call(
        hold_kernel,
        "hold",
        [SMEM] * 3 + [VMEM] * 3,
        [long_shard, shard, long_shard],
        1,
    )(*scalars, images, texts, near_0)
    near_1 = lax.ppermute(near_0, "inner", IMAGE_PAIRS)
    prior_0 = from_behind(texts_later, 1, within=True)
    after_0 = from_behind(images_later, -1, within=True)
    image_1 = gate(image_1, near_1)
    after_1 = gate(from_behind(image_1, -1), blocks=ROOM)
    prior_1 = gate(from_behind(text_1, 1), blocks=ROOM)
    edge = over_edge(gate(edge, image_1, text_1))

    image_part, text_part, loss_part, near_late = call(
        first_kernel, "first", [SMEM] * 3 + [VMEM] * 8, [real_shard, real_shard, line, int_line], 11
    )(*scalars, images, image_1, texts, text_1, prior_0, after_0, near_0, near_1)
    far_1 = from_behind(near_late, -1)
    image_send, loss_send = call(
        image_kernel, "image", [SMEM] * 3 + [VMEM] * 6, [shard, line], 2
    )(*scalars, image_1, prior_1, near_1, image_part, loss_part, edge)
    (text_send,) = call(
        text_kernel, "text", [SMEM] * 3 + [VMEM] * 5 + anywhere, [shard], 2
    )(*scalars, text_1, after_1, far_1, text_part, edge, image_send)
    image_own, text_own, loss_own = call(
        late_kernel,
        "late",
        [SMEM] * 3 + [VMEM] * 12 + anywhere,
        [real_shard, real_shard, line],
        15,
    )(
        *scalars,
        images,
        image_1,
        texts,
        text_1,
        prior_0,
        prior_1,
        after_0,
        after_1,
        near_0,
        near_1,
        far_1,
        edge,
        text_send,
    )

    image_back = lax.ppermute(image_send, "inner", IMAGE_PAIRS)
    text_back = lax.ppermute(text_send, "inner", TEXT_PAIRS)
    loss_back = lax.ppermute(loss_send, "inner", IMAGE_PAIRS)
    scale = logit_scale[0]
    loss_rows = (loss_own + loss_back)[0]
    image_grad = (scale * (image_own + image_back.astype(jnp.float32))).astype(jnp.bfloat16)
    text_grad = (scale * (text_own + text_back.astype(jnp.float32))).astype(jnp.bfloat16)
    return (loss_rows, image_grad, text_grad)


def solution(mesh):
    return jax.shard_map(
        per_device,
        mesh=mesh,
        in_specs=(
            P(("outer", "inner"), None),
            P(("outer", "inner"), None),
            P(("outer", "inner")),
            P(),
            P(),
        ),
        out_specs=(P(("outer", "inner")), P(("outer", "inner"), None), P(("outer", "inner"), None)),
        check_vma=False,
    )
```

```python
import jax
import jax.numpy as jnp
from jax import lax
from jax.experimental import pallas as pl
from jax.experimental.pallas import tpu as pltpu
from jax.sharding import PartitionSpec as P

IMAGE_PAIRS = [(0, 1), (1, 0), (2, 3), (3, 2)]
TEXT_PAIRS = [(1, 2), (2, 1), (3, 0), (0, 3)]

SHIFTS = (0, 8, 16)
TAIL = 16

VMEM = pl.BlockSpec(memory_space=pltpu.VMEM)
SMEM = pl.BlockSpec(memory_space=pltpu.SMEM)
LIMIT = 20 * 1024 * 1024
LATE_BLOCKS = 19


def from_behind(block, distance):
    count = lax.axis_size("outer")
    return lax.ppermute(block, "outer", [((i - distance) % count, i) for i in range(count)])


def over_last(x, y):
    return lax.dot_general(x, y, (((1,), (1,)), ((), ())), preferred_element_type=jnp.float32)


def over_first(x, y):
    return lax.dot_general(x, y, (((0,), (0,)), ((), ())), preferred_element_type=jnp.float32)


def hold_kernel(places, scale, bias, images, texts, positive, images_out, texts_out):
    rows = images.shape[0]
    images_out[pl.ds(0, rows), :] = images[...]
    images_out[pl.ds(rows, TAIL), :] = jnp.zeros((TAIL, images.shape[1]), jnp.bfloat16)
    digits = [(positive[...] >> shift) & 255 for shift in SHIFTS]
    digits = jnp.concatenate(digits + [jnp.zeros((TAIL - len(SHIFTS), rows), jnp.int32)])
    images_out[pl.ds(rows, TAIL), pl.ds(0, rows)] = digits.astype(jnp.float32).astype(jnp.bfloat16)
    texts_out[...] = texts[...]


class Blocks:
    def __init__(self, places, scale, bias):
        self.firsts, self.scale, self.bias = places, scale[0], bias[0]

    def logits(self, text, image, positive, first):
        logits = self.scale * over_last(text, image) + self.bias
        row = lax.broadcasted_iota(jnp.int32, logits.shape, 0)
        return logits, row == positive - self.firsts[first]

    def __call__(self, text, image, positive, first):
        logits, hits = self.logits(text, image, positive, first)
        decay = jnp.exp(-jnp.abs(logits))
        share = 1.0 / (1.0 + decay)
        sigmoid = jnp.where(logits >= 0.0, share, decay * share)
        weights = (sigmoid - hits.astype(jnp.float32)).astype(jnp.bfloat16)

        def loss():
            signed = jnp.where(hits, -logits, logits)
            return jnp.sum(jnp.maximum(signed, 0.0) + jnp.log1p(decay), axis=0, keepdims=True)

        return weights, loss


def read_after(after):
    rows = after.shape[0] - TAIL
    digits = after[pl.ds(rows, TAIL), pl.ds(0, rows)].astype(jnp.float32).astype(jnp.int32)
    far = sum(digits[k : k + 1, :] << shift for k, shift in enumerate(SHIFTS))
    return after[pl.ds(0, rows), :], far


def by_image(weights, image):
    return jnp.dot(weights, image, preferred_element_type=jnp.float32)


def gate_kernel(*refs):
    pass


def gate(array, *tokens):
    anywhere = pl.BlockSpec(memory_space=pl.ANY)
    return pl.pallas_call(
        gate_kernel,
        name="gate",
        out_shape=pltpu.VMEM(array.shape, array.dtype),
        in_specs=[anywhere] * (1 + len(tokens)),
        out_specs=anywhere,
        input_output_aliases={0: 0},
    )(pltpu.with_memory_space_constraint(array, pltpu.VMEM), *tokens)


def first_kernel(
    places,
    scale,
    bias,
    image_0,
    image_1,
    text_0,
    text_1,
    prior_0,
    after_0,
    near_0,
    near_1,
    image_part,
    text_part,
    near_out,
):
    near_out[...] = near_1[...]
    block = Blocks(places, scale, bias)
    weights, _ = block(text_1[...], image_1[...], near_1[...], 1)
    image_part[...] = over_first(weights, text_1[...])
    text_part[...] = by_image(weights, image_1[...])
    weights, _ = block(text_0[...], image_1[...], near_1[...], 0)
    image_part[...] += over_first(weights, text_0[...])
    weights, _ = block(text_1[...], image_0[...], near_0[...], 1)
    text_part[...] += by_image(weights, image_0[...])
    weights, _ = block(prior_0[...], image_1[...], near_1[...], 2)
    image_part[...] += over_first(weights, prior_0[...])
    image, far = read_after(after_0)
    weights, _ = block(text_1[...], image, far, 1)
    text_part[...] += by_image(weights, image)


def image_kernel(places, scale, bias, image_1, prior_1, near_1, image_part, image_send):
    weights, _ = Blocks(places, scale, bias)(prior_1[...], image_1[...], near_1[...], 3)
    total = image_part[...] + over_first(weights, prior_1[...])
    image_send[...] = total.astype(image_send.dtype)


def text_kernel(
    places,
    scale,
    bias,
    text_1,
    after_1,
    far_1,
    text_part,
    sent,
    text_send,
):
    block = Blocks(places, scale, bias)
    weights, _ = block(text_1[...], after_1[...], far_1[...], 1)
    total = text_part[...] + by_image(weights, after_1[...])
    text_send[...] = total.astype(text_send.dtype)


def late_kernel(
    places,
    scale,
    bias,
    image_0,
    image_1,
    text_0,
    text_1,
    prior_0,
    prior_1,
    after_0,
    after_1,
    near_0,
    near_1,
    far_1,
    sent,
    image_own,
    text_own,
    loss_own,
    loss_send,
):
    block = Blocks(places, scale, bias)
    rows = image_0.shape[0]
    weights, losses = block(text_0[...], image_0[...], near_0[...], 0)
    image_own[...] = over_first(weights, text_0[...])
    text_own[...] = by_image(weights, image_0[...])
    loss_own[...] = losses()

    def add_image(text, k):
        weights, losses = block(text, image_0[...], near_0[...], k)
        image_own[...] += over_first(weights, text)
        loss_own[...] += losses()

    def add_text(image, positive):
        weights, _ = block(text_0[...], image, positive, 0)
        text_own[...] += by_image(weights, image)

    add_image(text_1[...], 1)
    add_image(prior_1[...], 3)
    add_text(image_1[...], near_1[...])
    add_text(after_1[...], far_1[...])
    add_image(prior_0[...], 2)
    add_text(*read_after(after_0))
    loss_send[...] = jnp.zeros_like(loss_send)
    for k, text in enumerate((text_0, text_1, prior_0, prior_1)):
        _, losses = block(text[...], image_1[...], near_1[...], k)
        loss_send[...] += losses()


def cost(blocks):
    return pl.CostEstimate(
        flops=2 * blocks * 256 * 256 * 1152, bytes_accessed=1 << 20, transcendentals=0
    )


def call(kernel, name, in_specs, outs, blocks):
    return pl.pallas_call(
        kernel,
        name=name,
        out_shape=outs,
        in_specs=in_specs,
        out_specs=[VMEM] * len(outs),
        compiler_params=pltpu.CompilerParams(vmem_limit_bytes=LIMIT),
        cost_estimate=cost(blocks),
    )


def per_device(images, texts, positive, logit_scale, logit_bias):
    rows, width = texts.shape
    count = lax.axis_size("outer")
    group = lax.axis_index("outer")
    me = lax.axis_index("inner")
    whole = lax.axis_size("inner") * rows
    before = (group - 1 + count) % count
    places = jnp.stack(
        [
            group * whole + me * rows,
            group * whole + (3 - me) * rows,
            before * whole + me * rows,
            before * whole + (3 - me) * rows,
        ]
    ).astype(jnp.int32)
    scalars = (places, logit_scale, logit_bias)
    shard = jax.ShapeDtypeStruct((rows, width), jnp.bfloat16)
    long_shard = jax.ShapeDtypeStruct((rows + TAIL, width), jnp.bfloat16)
    real_shard = jax.ShapeDtypeStruct((rows, width), jnp.float32)
    line = jax.ShapeDtypeStruct((1, rows), jnp.float32)
    int_line = jax.ShapeDtypeStruct((1, rows), jnp.int32)
    anywhere = [pl.BlockSpec(memory_space=pl.ANY)]

    text_1 = lax.ppermute(texts, "inner", TEXT_PAIRS)
    image_1 = lax.ppermute(images, "inner", IMAGE_PAIRS)
    near_0 = positive[None, :]
    images_later, texts_later = call(
        hold_kernel,
        "hold",
        [SMEM] * 3 + [VMEM] * 3,
        [long_shard, shard],
        1,
    )(*scalars, images, texts, near_0)
    near_1 = lax.ppermute(near_0, "inner", IMAGE_PAIRS)
    prior_0 = from_behind(texts_later, 1)
    after_0 = from_behind(images_later, -1)
    image_1 = gate(image_1, near_1)
    after_1 = from_behind(image_1, -1)
    text_1 = gate(text_1, near_1)
    prior_1 = from_behind(text_1, 1)

    image_part, text_part, near_late = call(
        first_kernel, "first", [SMEM] * 3 + [VMEM] * 8, [real_shard, real_shard, int_line], 11
    )(*scalars, images, image_1, texts, text_1, prior_0, after_0, near_0, near_1)
    far_1 = from_behind(near_late, -1)
    (image_send,) = call(
        image_kernel, "image", [SMEM] * 3 + [VMEM] * 4, [shard], 2
    )(*scalars, image_1, prior_1, near_1, image_part)
    (text_send,) = call(
        text_kernel, "text", [SMEM] * 3 + [VMEM] * 4 + anywhere, [shard], 2
    )(*scalars, text_1, after_1, far_1, text_part, image_send)
    image_own, text_own, loss_own, loss_send = call(
        late_kernel,
        "late",
        [SMEM] * 3 + [VMEM] * 11 + anywhere,
        [real_shard, real_shard, line, line],
        LATE_BLOCKS,
    )(
        *scalars,
        images,
        image_1,
        texts,
        text_1,
        prior_0,
        prior_1,
        after_0,
        after_1,
        near_0,
        near_1,
        far_1,
            text_send,
    )

    image_back = lax.ppermute(image_send, "inner", IMAGE_PAIRS)
    text_back = lax.ppermute(text_send, "inner", TEXT_PAIRS)
    loss_back = lax.ppermute(loss_send, "inner", IMAGE_PAIRS)
    scale = logit_scale[0]
    loss_rows = (loss_own + loss_back)[0]
    image_grad = (scale * (image_own + image_back.astype(jnp.float32))).astype(jnp.bfloat16)
    text_grad = (scale * (text_own + text_back.astype(jnp.float32))).astype(jnp.bfloat16)
    return (loss_rows, image_grad, text_grad)


def solution(mesh):
    return jax.shard_map(
        per_device,
        mesh=mesh,
        in_specs=(
            P(("outer", "inner"), None),
            P(("outer", "inner"), None),
            P(("outer", "inner")),
            P(),
            P(),
        ),
        out_specs=(P(("outer", "inner")), P(("outer", "inner"), None), P(("outer", "inner"), None)),
        check_vma=False,
    )
```

```python
import jax
import jax.numpy as jnp
from jax import lax
from jax.experimental import pallas as pl
from jax.experimental.pallas import tpu as pltpu
from jax.sharding import PartitionSpec as P

IMAGE_PAIRS = [(0, 1), (1, 0), (2, 3), (3, 2)]
TEXT_PAIRS = [(1, 2), (2, 1), (3, 0), (0, 3)]

SHIFTS = (0, 8, 16)
TAIL = 16

VMEM = pl.BlockSpec(memory_space=pltpu.VMEM)
SMEM = pl.BlockSpec(memory_space=pltpu.SMEM)
LIMIT = 20 * 1024 * 1024
LATE_BLOCKS = 19


def from_behind(block, distance):
    count = lax.axis_size("outer")
    return lax.ppermute(block, "outer", [((i - distance) % count, i) for i in range(count)])


def over_last(x, y):
    return lax.dot_general(x, y, (((1,), (1,)), ((), ())), preferred_element_type=jnp.float32)


def over_first(x, y):
    return lax.dot_general(x, y, (((0,), (0,)), ((), ())), preferred_element_type=jnp.float32)


def hold_kernel(places, scale, bias, images, texts, positive, images_out, texts_out):
    rows = images.shape[0]
    images_out[pl.ds(0, rows), :] = images[...]
    images_out[pl.ds(rows, TAIL), :] = jnp.zeros((TAIL, images.shape[1]), jnp.bfloat16)
    digits = [(positive[...] >> shift) & 255 for shift in SHIFTS]
    digits = jnp.concatenate(digits + [jnp.zeros((TAIL - len(SHIFTS), rows), jnp.int32)])
    images_out[pl.ds(rows, TAIL), pl.ds(0, rows)] = digits.astype(jnp.float32).astype(jnp.bfloat16)
    texts_out[...] = texts[...]


class Blocks:
    def __init__(self, places, scale, bias):
        self.firsts, self.scale, self.bias = places, scale[0], bias[0]

    def logits(self, text, image, positive, first):
        logits = self.scale * over_last(text, image) + self.bias
        row = lax.broadcasted_iota(jnp.int32, logits.shape, 0)
        return logits, row == positive - self.firsts[first]

    def __call__(self, text, image, positive, first):
        logits, hits = self.logits(text, image, positive, first)
        decay = jnp.exp(-jnp.abs(logits))
        share = 1.0 / (1.0 + decay)
        sigmoid = jnp.where(logits >= 0.0, share, decay * share)
        weights = (sigmoid - hits.astype(jnp.float32)).astype(jnp.bfloat16)

        def loss():
            signed = jnp.where(hits, -logits, logits)
            return jnp.sum(jnp.maximum(signed, 0.0) + jnp.log1p(decay), axis=0, keepdims=True)

        return weights, loss


def read_after(after):
    rows = after.shape[0] - TAIL
    digits = after[pl.ds(rows, TAIL), pl.ds(0, rows)].astype(jnp.float32).astype(jnp.int32)
    far = sum(digits[k : k + 1, :] << shift for k, shift in enumerate(SHIFTS))
    return after[pl.ds(0, rows), :], far


def by_image(weights, image):
    return jnp.dot(weights, image, preferred_element_type=jnp.float32)


def gate_kernel(*refs):
    pass


def gate(array, *tokens):
    anywhere = pl.BlockSpec(memory_space=pl.ANY)
    return pl.pallas_call(
        gate_kernel,
        name="gate",
        out_shape=pltpu.VMEM(array.shape, array.dtype),
        in_specs=[anywhere] * (1 + len(tokens)),
        out_specs=anywhere,
        input_output_aliases={0: 0},
        cost_estimate=cost(0),
    )(pltpu.with_memory_space_constraint(array, pltpu.VMEM), *tokens)


def first_kernel(
    places,
    scale,
    bias,
    image_0,
    image_1,
    text_0,
    text_1,
    prior_0,
    after_0,
    near_0,
    near_1,
    image_part,
    text_part,
    near_out,
):
    near_out[...] = near_1[...]
    block = Blocks(places, scale, bias)
    weights, _ = block(text_1[...], image_1[...], near_1[...], 1)
    image_part[...] = over_first(weights, text_1[...])
    text_part[...] = by_image(weights, image_1[...])
    weights, _ = block(text_0[...], image_1[...], near_1[...], 0)
    image_part[...] += over_first(weights, text_0[...])
    weights, _ = block(text_1[...], image_0[...], near_0[...], 1)
    text_part[...] += by_image(weights, image_0[...])
    weights, _ = block(prior_0[...], image_1[...], near_1[...], 2)
    image_part[...] += over_first(weights, prior_0[...])
    image, far = read_after(after_0)
    weights, _ = block(text_1[...], image, far, 1)
    text_part[...] += by_image(weights, image)


def second_kernel(
    places,
    scale,
    bias,
    image_1,
    text_1,
    prior_1,
    after_1,
    near_1,
    far_1,
    image_part,
    text_part,
    image_send,
    text_send,
):
    block = Blocks(places, scale, bias)
    weights, _ = block(prior_1[...], image_1[...], near_1[...], 3)
    total = image_part[...] + over_first(weights, prior_1[...])
    image_send[...] = total.astype(image_send.dtype)
    weights, _ = block(text_1[...], after_1[...], far_1[...], 1)
    total = text_part[...] + by_image(weights, after_1[...])
    text_send[...] = total.astype(text_send.dtype)


def late_kernel(
    places,
    scale,
    bias,
    image_0,
    image_1,
    text_0,
    text_1,
    prior_0,
    prior_1,
    after_0,
    after_1,
    near_0,
    near_1,
    far_1,
    sent,
    image_own,
    text_own,
    loss_own,
    loss_send,
):
    block = Blocks(places, scale, bias)
    rows = image_0.shape[0]
    weights, losses = block(text_0[...], image_0[...], near_0[...], 0)
    image_own[...] = over_first(weights, text_0[...])
    text_own[...] = by_image(weights, image_0[...])
    loss_own[...] = losses()

    def add_image(text, k):
        weights, losses = block(text, image_0[...], near_0[...], k)
        image_own[...] += over_first(weights, text)
        loss_own[...] += losses()

    def add_text(image, positive):
        weights, _ = block(text_0[...], image, positive, 0)
        text_own[...] += by_image(weights, image)

    add_image(text_1[...], 1)
    add_image(prior_1[...], 3)
    add_text(image_1[...], near_1[...])
    add_text(after_1[...], far_1[...])
    add_image(prior_0[...], 2)
    add_text(*read_after(after_0))
    loss_send[...] = jnp.zeros_like(loss_send)
    for k, text in enumerate((text_0, text_1, prior_0, prior_1)):
        _, losses = block(text[...], image_1[...], near_1[...], k)
        loss_send[...] += losses()


def cost(blocks):
    return pl.CostEstimate(
        flops=2 * blocks * 256 * 256 * 1152, bytes_accessed=1 << 20, transcendentals=0
    )


def call(kernel, name, in_specs, outs, blocks):
    return pl.pallas_call(
        kernel,
        name=name,
        out_shape=outs,
        in_specs=in_specs,
        out_specs=[VMEM] * len(outs),
        compiler_params=pltpu.CompilerParams(vmem_limit_bytes=LIMIT),
        cost_estimate=cost(blocks),
    )


def per_device(images, texts, positive, logit_scale, logit_bias):
    rows, width = texts.shape
    count = lax.axis_size("outer")
    group = lax.axis_index("outer")
    me = lax.axis_index("inner")
    whole = lax.axis_size("inner") * rows
    before = (group - 1 + count) % count
    places = jnp.stack(
        [
            group * whole + me * rows,
            group * whole + (3 - me) * rows,
            before * whole + me * rows,
            before * whole + (3 - me) * rows,
        ]
    ).astype(jnp.int32)
    scalars = (places, logit_scale, logit_bias)
    shard = jax.ShapeDtypeStruct((rows, width), jnp.bfloat16)
    long_shard = jax.ShapeDtypeStruct((rows + TAIL, width), jnp.bfloat16)
    real_shard = jax.ShapeDtypeStruct((rows, width), jnp.float32)
    line = jax.ShapeDtypeStruct((1, rows), jnp.float32)
    int_line = jax.ShapeDtypeStruct((1, rows), jnp.int32)
    anywhere = [pl.BlockSpec(memory_space=pl.ANY)]

    text_1 = lax.ppermute(texts, "inner", TEXT_PAIRS)
    image_1 = lax.ppermute(images, "inner", IMAGE_PAIRS)
    near_0 = positive[None, :]
    images_later, texts_later = call(
        hold_kernel,
        "hold",
        [SMEM] * 3 + [VMEM] * 3,
        [long_shard, shard],
        1,
    )(*scalars, images, texts, near_0)
    near_1 = lax.ppermute(near_0, "inner", IMAGE_PAIRS)
    prior_0 = from_behind(texts_later, 1)
    after_0 = from_behind(images_later, -1)
    image_1 = gate(image_1, near_1)
    after_1 = from_behind(image_1, -1)
    text_1 = gate(text_1, near_1)
    prior_1 = from_behind(text_1, 1)

    image_part, text_part, near_late = call(
        first_kernel, "first", [SMEM] * 3 + [VMEM] * 8, [real_shard, real_shard, int_line], 11
    )(*scalars, images, image_1, texts, text_1, prior_0, after_0, near_0, near_1)
    far_1 = from_behind(near_late, -1)
    image_send, text_send = call(
        second_kernel, "second", [SMEM] * 3 + [VMEM] * 8, [shard, shard], 4
    )(*scalars, image_1, text_1, prior_1, after_1, near_1, far_1, image_part, text_part)
    image_own, text_own, loss_own, loss_send = call(
        late_kernel,
        "late",
        [SMEM] * 3 + [VMEM] * 11 + anywhere,
        [real_shard, real_shard, line, line],
        LATE_BLOCKS,
    )(
        *scalars,
        images,
        image_1,
        texts,
        text_1,
        prior_0,
        prior_1,
        after_0,
        after_1,
        near_0,
        near_1,
        far_1,
            text_send,
    )

    image_back = lax.ppermute(image_send, "inner", IMAGE_PAIRS)
    text_back = lax.ppermute(text_send, "inner", TEXT_PAIRS)
    loss_back = lax.ppermute(loss_send, "inner", IMAGE_PAIRS)
    scale = logit_scale[0]
    loss_rows = (loss_own + loss_back)[0]
    image_grad = (scale * (image_own + image_back.astype(jnp.float32))).astype(jnp.bfloat16)
    text_grad = (scale * (text_own + text_back.astype(jnp.float32))).astype(jnp.bfloat16)
    return (loss_rows, image_grad, text_grad)


def solution(mesh):
    return jax.shard_map(
        per_device,
        mesh=mesh,
        in_specs=(
            P(("outer", "inner"), None),
            P(("outer", "inner"), None),
            P(("outer", "inner")),
            P(),
            P(),
        ),
        out_specs=(P(("outer", "inner")), P(("outer", "inner"), None), P(("outer", "inner"), None)),
        check_vma=False,
    )
```

```python
import jax
import jax.numpy as jnp
from jax import lax
from jax.experimental import pallas as pl
from jax.experimental.pallas import tpu as pltpu
from jax.sharding import PartitionSpec as P

IMAGE_PAIRS = [(0, 1), (1, 0), (2, 3), (3, 2)]
TEXT_PAIRS = [(1, 2), (2, 1), (3, 0), (0, 3)]

SHIFTS = (0, 8, 16)
TAIL = 16

VMEM = pl.BlockSpec(memory_space=pltpu.VMEM)
SMEM = pl.BlockSpec(memory_space=pltpu.SMEM)
LIMIT = 20 * 1024 * 1024
LATE_BLOCKS = 19


def from_behind(block, distance):
    count = lax.axis_size("outer")
    return lax.ppermute(block, "outer", [((i - distance) % count, i) for i in range(count)])


def over_last(x, y):
    return lax.dot_general(x, y, (((1,), (1,)), ((), ())), preferred_element_type=jnp.float32)


def over_first(x, y):
    return lax.dot_general(x, y, (((0,), (0,)), ((), ())), preferred_element_type=jnp.float32)


def as_digits(positive):
    digits = [(positive >> shift) & 255 for shift in SHIFTS]
    digits.append(jnp.zeros((TAIL - len(SHIFTS), positive.shape[1]), jnp.int32))
    return jnp.concatenate(digits).astype(jnp.float32).astype(jnp.bfloat16)


def hold_kernel(places, scale, bias, images, texts, positive, images_out, texts_out):
    rows = images.shape[0]
    images_out[pl.ds(0, rows), :] = images[...]
    images_out[pl.ds(rows, TAIL), :] = jnp.zeros((TAIL, images.shape[1]), jnp.bfloat16)
    images_out[pl.ds(rows, TAIL), pl.ds(0, rows)] = as_digits(positive[...])
    texts_out[...] = texts[...]


def pack_kernel(image, positive, packed, tail, sems):
    rows = image.shape[0]
    body = pltpu.make_async_copy(image, packed.at[pl.ds(0, rows), :], sems.at[0])
    body.start()
    tail[...] = jnp.zeros_like(tail)
    tail[:, pl.ds(0, rows)] = as_digits(positive[...])
    end = pltpu.make_async_copy(tail, packed.at[pl.ds(rows, TAIL), :], sems.at[1])
    end.start()
    body.wait()
    end.wait()


def pack(image, positive):
    rows, width = image.shape
    anywhere = pl.BlockSpec(memory_space=pl.ANY)
    return pl.pallas_call(
        pack_kernel,
        name="pack",
        out_shape=pltpu.VMEM((rows + TAIL, width), image.dtype),
        in_specs=[anywhere, VMEM],
        out_specs=anywhere,
        scratch_shapes=[pltpu.VMEM((TAIL, width), image.dtype), pltpu.SemaphoreType.DMA((2,))],
        cost_estimate=cost(0),
    )(pltpu.with_memory_space_constraint(image, pltpu.VMEM), positive)


class Blocks:
    def __init__(self, places, scale, bias):
        self.firsts, self.scale, self.bias = places, scale[0], bias[0]

    def logits(self, text, image, positive, first):
        logits = self.scale * over_last(text, image) + self.bias
        row = lax.broadcasted_iota(jnp.int32, logits.shape, 0)
        return logits, row == positive - self.firsts[first]

    def __call__(self, text, image, positive, first):
        logits, hits = self.logits(text, image, positive, first)
        decay = jnp.exp(-jnp.abs(logits))
        share = 1.0 / (1.0 + decay)
        sigmoid = jnp.where(logits >= 0.0, share, decay * share)
        weights = (sigmoid - hits.astype(jnp.float32)).astype(jnp.bfloat16)

        def loss():
            signed = jnp.where(hits, -logits, logits)
            return jnp.sum(jnp.maximum(signed, 0.0) + jnp.log1p(decay), axis=0, keepdims=True)

        return weights, loss


def read_after(after):
    rows = after.shape[0] - TAIL
    digits = after[pl.ds(rows, TAIL), pl.ds(0, rows)].astype(jnp.float32).astype(jnp.int32)
    far = sum(digits[k : k + 1, :] << shift for k, shift in enumerate(SHIFTS))
    return after[pl.ds(0, rows), :], far


def by_image(weights, image):
    return jnp.dot(weights, image, preferred_element_type=jnp.float32)


def gate_kernel(*refs):
    pass


def gate(array, *tokens):
    anywhere = pl.BlockSpec(memory_space=pl.ANY)
    return pl.pallas_call(
        gate_kernel,
        name="gate",
        out_shape=pltpu.VMEM(array.shape, array.dtype),
        in_specs=[anywhere] * (1 + len(tokens)),
        out_specs=anywhere,
        input_output_aliases={0: 0},
        cost_estimate=cost(0),
    )(pltpu.with_memory_space_constraint(array, pltpu.VMEM), *tokens)


def first_kernel(
    places,
    scale,
    bias,
    image_0,
    image_1,
    text_0,
    text_1,
    prior_0,
    after_0,
    near_0,
    near_1,
    image_part,
    text_part,
):
    block = Blocks(places, scale, bias)
    weights, _ = block(text_1[...], image_1[...], near_1[...], 1)
    image_part[...] = over_first(weights, text_1[...])
    text_part[...] = by_image(weights, image_1[...])
    weights, _ = block(text_0[...], image_1[...], near_1[...], 0)
    image_part[...] += over_first(weights, text_0[...])
    weights, _ = block(text_1[...], image_0[...], near_0[...], 1)
    text_part[...] += by_image(weights, image_0[...])
    weights, _ = block(prior_0[...], image_1[...], near_1[...], 2)
    image_part[...] += over_first(weights, prior_0[...])
    image, far = read_after(after_0)
    weights, _ = block(text_1[...], image, far, 1)
    text_part[...] += by_image(weights, image)


def second_kernel(
    places,
    scale,
    bias,
    image_1,
    text_1,
    prior_1,
    after_1,
    near_1,
    image_part,
    text_part,
    image_send,
    text_send,
):
    block = Blocks(places, scale, bias)
    weights, _ = block(prior_1[...], image_1[...], near_1[...], 3)
    total = image_part[...] + over_first(weights, prior_1[...])
    image_send[...] = total.astype(image_send.dtype)
    image, far = read_after(after_1)
    weights, _ = block(text_1[...], image, far, 1)
    total = text_part[...] + by_image(weights, image)
    text_send[...] = total.astype(text_send.dtype)


def late_kernel(
    places,
    scale,
    bias,
    image_0,
    image_1,
    text_0,
    text_1,
    prior_0,
    prior_1,
    after_0,
    after_1,
    near_0,
    near_1,
    sent,
    image_own,
    text_own,
    loss_own,
    loss_send,
):
    block = Blocks(places, scale, bias)
    rows = image_0.shape[0]
    weights, losses = block(text_0[...], image_0[...], near_0[...], 0)
    image_own[...] = over_first(weights, text_0[...])
    text_own[...] = by_image(weights, image_0[...])
    loss_own[...] = losses()

    def add_image(text, k):
        weights, losses = block(text, image_0[...], near_0[...], k)
        image_own[...] += over_first(weights, text)
        loss_own[...] += losses()

    def add_text(image, positive):
        weights, _ = block(text_0[...], image, positive, 0)
        text_own[...] += by_image(weights, image)

    add_image(text_1[...], 1)
    add_image(prior_1[...], 3)
    add_text(image_1[...], near_1[...])
    add_text(*read_after(after_1))
    add_image(prior_0[...], 2)
    add_text(*read_after(after_0))
    loss_send[...] = jnp.zeros_like(loss_send)
    for k, text in enumerate((text_0, text_1, prior_0, prior_1)):
        _, losses = block(text[...], image_1[...], near_1[...], k)
        loss_send[...] += losses()


def cost(blocks):
    return pl.CostEstimate(
        flops=2 * blocks * 256 * 256 * 1152, bytes_accessed=1 << 20, transcendentals=0
    )


def call(kernel, name, in_specs, outs, blocks):
    return pl.pallas_call(
        kernel,
        name=name,
        out_shape=outs,
        in_specs=in_specs,
        out_specs=[VMEM] * len(outs),
        compiler_params=pltpu.CompilerParams(vmem_limit_bytes=LIMIT),
        cost_estimate=cost(blocks),
    )


def per_device(images, texts, positive, logit_scale, logit_bias):
    rows, width = texts.shape
    count = lax.axis_size("outer")
    group = lax.axis_index("outer")
    me = lax.axis_index("inner")
    whole = lax.axis_size("inner") * rows
    before = (group - 1 + count) % count
    places = jnp.stack(
        [
            group * whole + me * rows,
            group * whole + (3 - me) * rows,
            before * whole + me * rows,
            before * whole + (3 - me) * rows,
        ]
    ).astype(jnp.int32)
    scalars = (places, logit_scale, logit_bias)
    shard = jax.ShapeDtypeStruct((rows, width), jnp.bfloat16)
    long_shard = jax.ShapeDtypeStruct((rows + TAIL, width), jnp.bfloat16)
    real_shard = jax.ShapeDtypeStruct((rows, width), jnp.float32)
    line = jax.ShapeDtypeStruct((1, rows), jnp.float32)
    anywhere = [pl.BlockSpec(memory_space=pl.ANY)]

    text_1 = lax.ppermute(texts, "inner", TEXT_PAIRS)
    image_1 = lax.ppermute(images, "inner", IMAGE_PAIRS)
    near_0 = positive[None, :]
    images_later, texts_later = call(
        hold_kernel,
        "hold",
        [SMEM] * 3 + [VMEM] * 3,
        [long_shard, shard],
        1,
    )(*scalars, images, texts, near_0)
    near_1 = lax.ppermute(near_0, "inner", IMAGE_PAIRS)
    prior_0 = from_behind(texts_later, 1)
    after_0 = from_behind(images_later, -1)
    after_1 = from_behind(pack(image_1, near_1), -1)
    text_1 = gate(text_1, near_1)
    prior_1 = from_behind(text_1, 1)

    image_part, text_part = call(
        first_kernel, "first", [SMEM] * 3 + [VMEM] * 8, [real_shard, real_shard], 11
    )(*scalars, images, image_1, texts, text_1, prior_0, after_0, near_0, near_1)
    image_send, text_send = call(
        second_kernel, "second", [SMEM] * 3 + [VMEM] * 7, [shard, shard], 4
    )(*scalars, image_1, text_1, prior_1, after_1, near_1, image_part, text_part)
    image_own, text_own, loss_own, loss_send = call(
        late_kernel,
        "late",
        [SMEM] * 3 + [VMEM] * 10 + anywhere,
        [real_shard, real_shard, line, line],
        LATE_BLOCKS,
    )(
        *scalars,
        images,
        image_1,
        texts,
        text_1,
        prior_0,
        prior_1,
        after_0,
        after_1,
        near_0,
        near_1,
            text_send,
    )

    image_back = lax.ppermute(image_send, "inner", IMAGE_PAIRS)
    text_back = lax.ppermute(text_send, "inner", TEXT_PAIRS)
    loss_back = lax.ppermute(loss_send, "inner", IMAGE_PAIRS)
    scale = logit_scale[0]
    loss_rows = (loss_own + loss_back)[0]
    image_grad = (scale * (image_own + image_back.astype(jnp.float32))).astype(jnp.bfloat16)
    text_grad = (scale * (text_own + text_back.astype(jnp.float32))).astype(jnp.bfloat16)
    return (loss_rows, image_grad, text_grad)


def solution(mesh):
    return jax.shard_map(
        per_device,
        mesh=mesh,
        in_specs=(
            P(("outer", "inner"), None),
            P(("outer", "inner"), None),
            P(("outer", "inner")),
            P(),
            P(),
        ),
        out_specs=(P(("outer", "inner")), P(("outer", "inner"), None), P(("outer", "inner"), None)),
        check_vma=False,
    )
```

```python
import jax
import jax.numpy as jnp
from jax import lax
from jax.experimental import pallas as pl
from jax.experimental.pallas import tpu as pltpu
from jax.sharding import PartitionSpec as P

IMAGE_PAIRS = [(0, 1), (1, 0), (2, 3), (3, 2)]
TEXT_PAIRS = [(1, 2), (2, 1), (3, 0), (0, 3)]

SHIFTS = (0, 8, 16)
TAIL = 16

VMEM = pl.BlockSpec(memory_space=pltpu.VMEM)
SMEM = pl.BlockSpec(memory_space=pltpu.SMEM)
LIMIT = 20 * 1024 * 1024
LATE_BLOCKS = 19
PLANES = 3


def from_behind(block, distance):
    count = lax.axis_size("outer")
    return lax.ppermute(block, "outer", [((i - distance) % count, i) for i in range(count)])


def credit_from_edge(block):
    count = lax.axis_size("outer")
    plane = count // PLANES
    firsts = range(0, count, plane)
    pairs = [(k, k + 1) for k in firsts] + [(k + plane - 1, k + plane - 2) for k in firsts]
    return lax.ppermute(block, "outer", pairs)


def over_last(x, y):
    return lax.dot_general(x, y, (((1,), (1,)), ((), ())), preferred_element_type=jnp.float32)


def over_first(x, y):
    return lax.dot_general(x, y, (((0,), (0,)), ((), ())), preferred_element_type=jnp.float32)


def as_digits(positive):
    digits = [(positive >> shift) & 255 for shift in SHIFTS]
    digits.append(jnp.zeros((TAIL - len(SHIFTS), positive.shape[1]), jnp.int32))
    return jnp.concatenate(digits).astype(jnp.float32).astype(jnp.bfloat16)


def hold_kernel(places, scale, bias, images, texts, positive, images_out, texts_out):
    rows = images.shape[0]
    images_out[pl.ds(0, rows), :] = images[...]
    images_out[pl.ds(rows, TAIL), :] = jnp.zeros((TAIL, images.shape[1]), jnp.bfloat16)
    images_out[pl.ds(rows, TAIL), pl.ds(0, rows)] = as_digits(positive[...])
    texts_out[...] = texts[...]


def note_kernel(line, first, second, line_out):
    line_out[...] = line[...]


def pack_kernel(image, positive, packed, tail, sems):
    rows = image.shape[0]
    body = pltpu.make_async_copy(image, packed.at[pl.ds(0, rows), :], sems.at[0])
    body.start()
    tail[...] = jnp.zeros_like(tail)
    tail[:, pl.ds(0, rows)] = as_digits(positive[...])
    end = pltpu.make_async_copy(tail, packed.at[pl.ds(rows, TAIL), :], sems.at[1])
    end.start()
    body.wait()
    end.wait()


def pack(image, positive):
    rows, width = image.shape
    anywhere = pl.BlockSpec(memory_space=pl.ANY)
    return pl.pallas_call(
        pack_kernel,
        name="pack",
        out_shape=pltpu.VMEM((rows + TAIL, width), image.dtype),
        in_specs=[anywhere, VMEM],
        out_specs=anywhere,
        scratch_shapes=[pltpu.VMEM((TAIL, width), image.dtype), pltpu.SemaphoreType.DMA((2,))],
        cost_estimate=cost(0),
    )(pltpu.with_memory_space_constraint(image, pltpu.VMEM), positive)


class Blocks:
    def __init__(self, places, scale, bias):
        self.firsts, self.scale, self.bias = places, scale[0], bias[0]

    def logits(self, text, image, positive, first):
        logits = self.scale * over_last(text, image) + self.bias
        row = lax.broadcasted_iota(jnp.int32, logits.shape, 0)
        return logits, row == positive - self.firsts[first]

    def __call__(self, text, image, positive, first):
        logits, hits = self.logits(text, image, positive, first)
        decay = jnp.exp(-jnp.abs(logits))
        share = 1.0 / (1.0 + decay)
        sigmoid = jnp.where(logits >= 0.0, share, decay * share)
        weights = (sigmoid - hits.astype(jnp.float32)).astype(jnp.bfloat16)

        def loss():
            signed = jnp.where(hits, -logits, logits)
            return jnp.sum(jnp.maximum(signed, 0.0) + jnp.log1p(decay), axis=0, keepdims=True)

        return weights, loss


def read_after(after):
    rows = after.shape[0] - TAIL
    digits = after[pl.ds(rows, TAIL), pl.ds(0, rows)].astype(jnp.float32).astype(jnp.int32)
    far = sum(digits[k : k + 1, :] << shift for k, shift in enumerate(SHIFTS))
    return after[pl.ds(0, rows), :], far


def by_image(weights, image):
    return jnp.dot(weights, image, preferred_element_type=jnp.float32)


def gate_kernel(*refs):
    pass


def gate(array, *tokens):
    anywhere = pl.BlockSpec(memory_space=pl.ANY)
    return pl.pallas_call(
        gate_kernel,
        name="gate",
        out_shape=pltpu.VMEM(array.shape, array.dtype),
        in_specs=[anywhere] * (1 + len(tokens)),
        out_specs=anywhere,
        input_output_aliases={0: 0},
        cost_estimate=cost(0),
    )(pltpu.with_memory_space_constraint(array, pltpu.VMEM), *tokens)


def first_kernel(
    places,
    scale,
    bias,
    image_0,
    image_1,
    text_0,
    text_1,
    prior_0,
    after_0,
    near_0,
    near_1,
    image_part,
    text_part,
):
    block = Blocks(places, scale, bias)
    weights, _ = block(text_1[...], image_1[...], near_1[...], 1)
    image_part[...] = over_first(weights, text_1[...])
    text_part[...] = by_image(weights, image_1[...])
    weights, _ = block(text_0[...], image_1[...], near_1[...], 0)
    image_part[...] += over_first(weights, text_0[...])
    weights, _ = block(text_1[...], image_0[...], near_0[...], 1)
    text_part[...] += by_image(weights, image_0[...])
    weights, _ = block(prior_0[...], image_1[...], near_1[...], 2)
    image_part[...] += over_first(weights, prior_0[...])
    image, far = read_after(after_0)
    weights, _ = block(text_1[...], image, far, 1)
    text_part[...] += by_image(weights, image)


def second_kernel(
    places,
    scale,
    bias,
    image_1,
    text_1,
    prior_1,
    after_1,
    near_1,
    image_part,
    text_part,
    image_send,
    text_send,
):
    block = Blocks(places, scale, bias)
    weights, _ = block(prior_1[...], image_1[...], near_1[...], 3)
    total = image_part[...] + over_first(weights, prior_1[...])
    image_send[...] = total.astype(image_send.dtype)
    image, far = read_after(after_1)
    weights, _ = block(text_1[...], image, far, 1)
    total = text_part[...] + by_image(weights, image)
    text_send[...] = total.astype(text_send.dtype)


def late_kernel(
    places,
    scale,
    bias,
    image_0,
    image_1,
    text_0,
    text_1,
    prior_0,
    prior_1,
    after_0,
    after_1,
    near_0,
    near_1,
    sent,
    image_own,
    text_own,
    loss_own,
    loss_send,
):
    block = Blocks(places, scale, bias)
    rows = image_0.shape[0]
    weights, losses = block(text_0[...], image_0[...], near_0[...], 0)
    image_own[...] = over_first(weights, text_0[...])
    text_own[...] = by_image(weights, image_0[...])
    loss_own[...] = losses()

    def add_image(text, k):
        weights, losses = block(text, image_0[...], near_0[...], k)
        image_own[...] += over_first(weights, text)
        loss_own[...] += losses()

    def add_text(image, positive):
        weights, _ = block(text_0[...], image, positive, 0)
        text_own[...] += by_image(weights, image)

    add_image(text_1[...], 1)
    add_image(prior_1[...], 3)
    add_text(image_1[...], near_1[...])
    add_text(*read_after(after_1))
    add_image(prior_0[...], 2)
    add_text(*read_after(after_0))
    loss_send[...] = jnp.zeros_like(loss_send)
    for k, text in enumerate((text_0, text_1, prior_0, prior_1)):
        _, losses = block(text[...], image_1[...], near_1[...], k)
        loss_send[...] += losses()


def cost(blocks):
    return pl.CostEstimate(
        flops=2 * blocks * 256 * 256 * 1152, bytes_accessed=1 << 20, transcendentals=0
    )


def call(kernel, name, in_specs, outs, blocks):
    return pl.pallas_call(
        kernel,
        name=name,
        out_shape=outs,
        in_specs=in_specs,
        out_specs=[VMEM] * len(outs),
        compiler_params=pltpu.CompilerParams(vmem_limit_bytes=LIMIT),
        cost_estimate=cost(blocks),
    )


def per_device(images, texts, positive, logit_scale, logit_bias):
    rows, width = texts.shape
    count = lax.axis_size("outer")
    group = lax.axis_index("outer")
    me = lax.axis_index("inner")
    whole = lax.axis_size("inner") * rows
    before = (group - 1 + count) % count
    places = jnp.stack(
        [
            group * whole + me * rows,
            group * whole + (3 - me) * rows,
            before * whole + me * rows,
            before * whole + (3 - me) * rows,
        ]
    ).astype(jnp.int32)
    scalars = (places, logit_scale, logit_bias)
    shard = jax.ShapeDtypeStruct((rows, width), jnp.bfloat16)
    long_shard = jax.ShapeDtypeStruct((rows + TAIL, width), jnp.bfloat16)
    real_shard = jax.ShapeDtypeStruct((rows, width), jnp.float32)
    line = jax.ShapeDtypeStruct((1, rows), jnp.float32)
    int_line = jax.ShapeDtypeStruct((1, rows), jnp.int32)
    anywhere = [pl.BlockSpec(memory_space=pl.ANY)]

    text_1 = lax.ppermute(texts, "inner", TEXT_PAIRS)
    image_1 = lax.ppermute(images, "inner", IMAGE_PAIRS)
    near_0 = positive[None, :]
    images_later, texts_later = call(
        hold_kernel,
        "hold",
        [SMEM] * 3 + [VMEM] * 3,
        [long_shard, shard],
        1,
    )(*scalars, images, texts, near_0)
    near_1 = lax.ppermute(near_0, "inner", IMAGE_PAIRS)
    prior_0 = from_behind(texts_later, 1)
    after_0 = from_behind(images_later, -1)
    after_1 = from_behind(pack(image_1, near_1), -1)
    text_1 = gate(text_1, near_1)
    prior_1 = from_behind(text_1, 1)

    image_part, text_part = call(
        first_kernel, "first", [SMEM] * 3 + [VMEM] * 8, [real_shard, real_shard], 11
    )(*scalars, images, image_1, texts, text_1, prior_0, after_0, near_0, near_1)
    image_send, text_send = call(
        second_kernel, "second", [SMEM] * 3 + [VMEM] * 7, [shard, shard], 4
    )(*scalars, image_1, text_1, prior_1, after_1, near_1, image_part, text_part)
    (note,) = call(note_kernel, "note", [VMEM] + anywhere * 2, [int_line], 0)(
        near_1, after_1, prior_1
    )
    credit = credit_from_edge(note)
    image_send, text_send = gate(image_send, credit), gate(text_send, credit)
    image_own, text_own, loss_own, loss_send = call(
        late_kernel,
        "late",
        [SMEM] * 3 + [VMEM] * 10 + anywhere,
        [real_shard, real_shard, line, line],
        LATE_BLOCKS,
    )(
        *scalars,
        images,
        image_1,
        texts,
        text_1,
        prior_0,
        prior_1,
        after_0,
        after_1,
        near_0,
        near_1,
            text_send,
    )

    image_back = lax.ppermute(image_send, "inner", IMAGE_PAIRS)
    text_back = lax.ppermute(text_send, "inner", TEXT_PAIRS)
    loss_back = lax.ppermute(loss_send, "inner", IMAGE_PAIRS)
    scale = logit_scale[0]
    loss_rows = (loss_own + loss_back)[0]
    image_grad = (scale * (image_own + image_back.astype(jnp.float32))).astype(jnp.bfloat16)
    text_grad = (scale * (text_own + text_back.astype(jnp.float32))).astype(jnp.bfloat16)
    return (loss_rows, image_grad, text_grad)


def solution(mesh):
    return jax.shard_map(
        per_device,
        mesh=mesh,
        in_specs=(
            P(("outer", "inner"), None),
            P(("outer", "inner"), None),
            P(("outer", "inner")),
            P(),
            P(),
        ),
        out_specs=(P(("outer", "inner")), P(("outer", "inner"), None), P(("outer", "inner"), None)),
        check_vma=False,
    )
```

```python
import jax
import jax.numpy as jnp
from jax import lax
from jax.experimental import pallas as pl
from jax.experimental.pallas import tpu as pltpu
from jax.sharding import PartitionSpec as P

IMAGE_PAIRS = [(0, 1), (1, 0), (2, 3), (3, 2)]
TEXT_PAIRS = [(1, 2), (2, 1), (3, 0), (0, 3)]

SHIFTS = (0, 8, 16)
TAIL = 16

VMEM = pl.BlockSpec(memory_space=pltpu.VMEM)
SMEM = pl.BlockSpec(memory_space=pltpu.SMEM)
LIMIT = 20 * 1024 * 1024


def from_behind(block, distance):
    count = lax.axis_size("outer")
    return lax.ppermute(block, "outer", [((i - distance) % count, i) for i in range(count)])


def over_last(x, y):
    return lax.dot_general(x, y, (((1,), (1,)), ((), ())), preferred_element_type=jnp.float32)


def over_first(x, y):
    return lax.dot_general(x, y, (((0,), (0,)), ((), ())), preferred_element_type=jnp.float32)


def hold_kernel(firsts, reals, images, texts, positive, images_out, texts_out):
    rows = images.shape[0]
    images_out[pl.ds(0, rows), :] = images[...]
    images_out[pl.ds(rows, TAIL), :] = jnp.zeros((TAIL, images.shape[1]), jnp.bfloat16)
    digits = [(positive[...] >> shift) & 255 for shift in SHIFTS]
    digits = jnp.concatenate(digits + [jnp.zeros((TAIL - len(SHIFTS), rows), jnp.int32)])
    images_out[pl.ds(rows, TAIL), pl.ds(0, rows)] = digits.astype(jnp.float32).astype(jnp.bfloat16)
    texts_out[...] = texts[...]


class Blocks:
    def __init__(self, firsts, reals):
        self.firsts, self.scale, self.bias = firsts, reals[0], reals[1]

    def logits(self, text, image, positive, first):
        logits = self.scale * over_last(text, image) + self.bias
        row = lax.broadcasted_iota(jnp.int32, logits.shape, 0)
        return logits, row == positive - self.firsts[first]

    def __call__(self, text, image, positive, first):
        logits, hits = self.logits(text, image, positive, first)
        decay = jnp.exp(-jnp.abs(logits))
        share = 1.0 / (1.0 + decay)
        sigmoid = jnp.where(logits >= 0.0, share, decay * share)
        weights = (sigmoid - hits.astype(jnp.float32)).astype(jnp.bfloat16)

        def loss():
            signed = jnp.where(hits, -logits, logits)
            return jnp.sum(jnp.maximum(signed, 0.0) + jnp.log1p(decay), axis=0, keepdims=True)

        return weights, loss


def read_after(after):
    rows = after.shape[0] - TAIL
    digits = after[pl.ds(rows, TAIL), pl.ds(0, rows)].astype(jnp.float32).astype(jnp.int32)
    far = sum(digits[k : k + 1, :] << shift for k, shift in enumerate(SHIFTS))
    return after[pl.ds(0, rows), :], far


def by_image(weights, image):
    return jnp.dot(weights, image, preferred_element_type=jnp.float32)


def gate_kernel(*refs):
    pass


def gate(array, *tokens):
    anywhere = pl.BlockSpec(memory_space=pl.ANY)
    return pl.pallas_call(
        gate_kernel,
        name="gate",
        out_shape=pltpu.VMEM(array.shape, array.dtype),
        in_specs=[anywhere] * (1 + len(tokens)),
        out_specs=anywhere,
        input_output_aliases={0: 0},
    )(pltpu.with_memory_space_constraint(array, pltpu.VMEM), *tokens)


def first_kernel(
    firsts,
    reals,
    image_0,
    image_1,
    text_0,
    text_1,
    prior_0,
    after_0,
    near_0,
    near_1,
    image_part,
    text_part,
    loss_part,
):
    block = Blocks(firsts, reals)
    weights, losses = block(text_1[...], image_1[...], near_1[...], 1)
    image_part[...] = over_first(weights, text_1[...])
    text_part[...] = by_image(weights, image_1[...])
    loss_part[...] = losses()
    weights, losses = block(text_0[...], image_1[...], near_1[...], 0)
    image_part[...] += over_first(weights, text_0[...])
    loss_part[...] += losses()
    weights, losses = block(prior_0[...], image_1[...], near_1[...], 2)
    image_part[...] += over_first(weights, prior_0[...])
    loss_part[...] += losses()
    weights, _ = block(text_1[...], image_0[...], near_0[...], 1)
    text_part[...] += by_image(weights, image_0[...])
    image, far = read_after(after_0)
    weights, _ = block(text_1[...], image, far, 1)
    text_part[...] += by_image(weights, image)


def text_kernel(firsts, reals, text_1, after_1, far_1, text_part, text_send):
    weights, _ = Blocks(firsts, reals)(text_1[...], after_1[...], far_1[...], 1)
    total = text_part[...] + by_image(weights, after_1[...])
    text_send[...] = total.astype(text_send.dtype)


def image_kernel(
    firsts, reals, image_1, prior_1, near_1, image_part, loss_part, sent, image_send, loss_send
):
    weights, losses = Blocks(firsts, reals)(prior_1[...], image_1[...], near_1[...], 3)
    total = image_part[...] + over_first(weights, prior_1[...])
    image_send[...] = total.astype(image_send.dtype)
    loss_send[...] = loss_part[...] + losses()


def late_kernel(
    firsts,
    reals,
    image_0,
    image_1,
    text_0,
    text_1,
    prior_0,
    prior_1,
    after_0,
    after_1,
    near_0,
    near_1,
    far_1,
    image_sent,
    image_own,
    text_own,
    loss_own,
):
    block = Blocks(firsts, reals)
    weights, losses = block(text_0[...], image_0[...], near_0[...], 0)
    image_own[...] = over_first(weights, text_0[...])
    text_own[...] = by_image(weights, image_0[...])
    loss_own[...] = losses()
    for k, text in ((1, text_1), (2, prior_0), (3, prior_1)):
        weights, losses = block(text[...], image_0[...], near_0[...], k)
        image_own[...] += over_first(weights, text[...])
        loss_own[...] += losses()
    after, far = read_after(after_0)
    for image, positive in ((image_1[...], near_1[...]), (after, far), (after_1[...], far_1[...])):
        weights, _ = block(text_0[...], image, positive, 0)
        text_own[...] += by_image(weights, image)


def call(kernel, name, in_specs, outs, blocks):
    return pl.pallas_call(
        kernel,
        name=name,
        out_shape=outs,
        in_specs=in_specs,
        out_specs=[VMEM] * len(outs),
        compiler_params=pltpu.CompilerParams(vmem_limit_bytes=LIMIT),
        cost_estimate=pl.CostEstimate(
            flops=2 * blocks * 256 * 256 * 1152, bytes_accessed=1 << 20, transcendentals=0
        ),
    )


def per_device(images, texts, positive, logit_scale, logit_bias):
    rows, width = texts.shape
    count = lax.axis_size("outer")
    group = lax.axis_index("outer")
    me = lax.axis_index("inner")
    whole = lax.axis_size("inner") * rows
    before = (group - 1 + count) % count
    firsts = jnp.stack(
        [
            group * whole + me * rows,
            group * whole + (3 - me) * rows,
            before * whole + me * rows,
            before * whole + (3 - me) * rows,
        ]
    ).astype(jnp.int32)
    reals = jnp.concatenate([logit_scale, logit_bias])
    shard = jax.ShapeDtypeStruct((rows, width), jnp.bfloat16)
    long_shard = jax.ShapeDtypeStruct((rows + TAIL, width), jnp.bfloat16)
    real_shard = jax.ShapeDtypeStruct((rows, width), jnp.float32)
    line = jax.ShapeDtypeStruct((1, rows), jnp.float32)

    text_1 = lax.ppermute(texts, "inner", TEXT_PAIRS)
    image_1 = lax.ppermute(images, "inner", IMAGE_PAIRS)
    near_0 = positive[None, :]
    images_later, texts_later = call(
        hold_kernel, "hold", [SMEM] * 2 + [VMEM] * 3, [long_shard, shard], 1
    )(firsts, reals, images, texts, near_0)
    near_1 = lax.ppermute(near_0, "inner", IMAGE_PAIRS)
    prior_0 = from_behind(texts_later, 1)
    after_0 = from_behind(images_later, -1)
    image_1 = gate(image_1, near_1)
    after_1 = from_behind(image_1, -1)
    prior_1 = from_behind(text_1, 1)
    far_1 = from_behind(near_1, -1)

    image_part, text_part, loss_part = call(
        first_kernel, "first", [SMEM] * 2 + [VMEM] * 8, [real_shard, real_shard, line], 11
    )(firsts, reals, images, image_1, texts, text_1, prior_0, after_0, near_0, near_1)
    (text_send,) = call(text_kernel, "text", [SMEM] * 2 + [VMEM] * 4, [shard], 2)(
        firsts, reals, text_1, after_1, far_1, text_part
    )
    image_send, loss_send = call(image_kernel, "image", [SMEM] * 2 + [VMEM] * 5 + [pl.BlockSpec(memory_space=pl.ANY)], [shard, line], 2)(
        firsts, reals, image_1, prior_1, near_1, image_part, loss_part, text_send
    )
    image_own, text_own, loss_own = call(
        late_kernel,
        "late",
        [SMEM] * 2 + [VMEM] * 11 + [pl.BlockSpec(memory_space=pl.ANY)],
        [real_shard, real_shard, line],
        15,
    )(
        firsts,
        reals,
        images,
        image_1,
        texts,
        text_1,
        prior_0,
        prior_1,
        after_0,
        after_1,
        near_0,
        near_1,
        far_1,
        image_send,
    )
    image_back = lax.ppermute(image_send, "inner", IMAGE_PAIRS)
    text_back = lax.ppermute(text_send, "inner", TEXT_PAIRS)
    loss_back = lax.ppermute(loss_send, "inner", IMAGE_PAIRS)
    scale = logit_scale[0]
    loss_rows = (loss_own + loss_back)[0]
    image_grad = (scale * (image_own + image_back.astype(jnp.float32))).astype(jnp.bfloat16)
    text_grad = (scale * (text_own + text_back.astype(jnp.float32))).astype(jnp.bfloat16)
    return (loss_rows, image_grad, text_grad)


def solution(mesh):
    return jax.shard_map(
        per_device,
        mesh=mesh,
        in_specs=(
            P(("outer", "inner"), None),
            P(("outer", "inner"), None),
            P(("outer", "inner")),
            P(),
            P(),
        ),
        out_specs=(P(("outer", "inner")), P(("outer", "inner"), None), P(("outer", "inner"), None)),
        check_vma=False,
    )
```
